512 devices in a mesh: rep: 16 (over y, x), dom: 32 (over z, core).
Axes of the slice: x: 4, y: 4, z: 16, core: 2. Of those that a mesh axis runs over, the one named last changes fastest.
Arguments:
- positions: float32 [16, 3, 32768], P('rep', None, 'dom'), may hold values from -6 to 6
- velocities: float32 [16, 3, 32768], P('rep', None, 'dom'), may hold values from -6 to 6
- charge: float32 [32768], P('dom'), may hold values from 0.5 to 2
- inverse_mass: float32 [32768], P('dom'), may hold values from 0.5 to 2
- pair_tiles: int32 [256, 6], P('dom'), may hold values from -1 to 11, as said below
- halo_tiles: int32 [32, 2, 2], P('dom'), may hold values from 0 to 7, as said below
- owners: int32 [256, 4], P('dom'), may hold values from 0 to 31, all different within a row; in each aligned block of 8 rows (0 to 7, 8 to 15, ...) at most 2 rows name the same one
- centres: float32 [3, 32768], P(None, 'dom'), may hold values from -6 to 6
- widths: float32 [32768], P('dom'), may hold values from 1 to 4
- map_density: float32 [32768], P('dom'), may hold values from 0.1 to 0.6
- map_error: float32 [32768], P('dom'), may hold values from 0.1 to 0.3
- partner: int32 [16], replicated, may hold values from 0 to 15, as said below
- decision: int32 [16], replicated, may hold values from 0 to 1, as said below
Outputs:
- new_positions: float32 [16, 3, 32768], P('rep', None, 'dom')
- new_velocities: float32 [16, 3, 32768], P('rep', None, 'dom')
- model_map: float32 [32768], P('dom')
The draws below stay inside these ranges and needn't reach their ends.
Inputs may be any that keep to these rules, and one draw needn't show every extreme that they name: `pair_tiles`: entry j of a tile's row names tile j of the same domain if j < 8; tile j - 8 of the upper list (row [d - 1, 1]) of the domain below if j < 10; else tile j - 10 of the lower list (row [d + 1, 0]) of the domain above; domains wrap around. -1 marks an empty entry; live entries of a row are distinct and come first. `halo_tiles`: row [d, 0] lists distinct tiles of domain d for domain d - 1, row [d, 1] distinct tiles for domain d + 1. `owners`: each row names 4 distinct domains; within the 8 rows of one domain no domain is named more than 2 times, a bound that some block reaches. `partner`: a permutation of the replicas; some replica r has partner r + 16 / 2 (counted round) and decision 1. `decision`: the same on all replicas of one cycle of partner; at least one replica is accepted and one is not.
All inputs are finite; a program needn't handle non-finite values.
Results may differ from the reference program's by a relative error of at most 0.0001.
Values sent between devices are 32-bit elements; how exact they have to be, the bound alone decides.
A program may use at most 64 MiB of HBM per device.

```python
import math
import jax
import jax.numpy as jnp
import numpy as np
from jax import lax

TILE = 128
NB = 6
OWN = 4
STEPS = 2
NT = 8
COMP_DEV = 1024
REPS = 16
DOMS = 32
HALO_T = 2
CAP = 2
ATOMS = 32768
COMPS = 32768


def draw_halo_tiles(key, part):
    scores = jax.random.randint(key, (DOMS, 2, NT), 0, 65536) * NT + jnp.arange(NT, dtype=jnp.int32)
    ordering = jnp.argsort(scores, axis=-1)
    return ordering[:, :, :HALO_T].astype(jnp.int32)


def draw_pair_tiles(key, part):
    extent = NT + 2 * HALO_T
    row_count = DOMS * NT
    first_key, second_key = jax.random.split(key)
    scores = jax.random.randint(first_key, (row_count, extent), 0, 65536) * extent + jnp.arange(extent, dtype=jnp.int32)
    row_ids = jnp.arange(row_count, dtype=jnp.int32)
    column_ids = jnp.arange(extent, dtype=jnp.int32)
    leading = (row_ids[:, None] % NT == 0) & (column_ids[None, :] == extent - 1)
    lowered = (row_ids[:, None] % NT == 1) & (column_ids[None, :] == NT)
    scores = jnp.where(leading | lowered, -1, scores)
    chosen = jnp.argsort(scores, axis=-1)[:, :NB].astype(jnp.int32)
    live_count = jax.random.randint(second_key, (row_count,), max(1, NB // 2), NB + 1)
    live_count = jnp.where(row_ids % NT == 0, NB, live_count)
    live_count = jnp.where(row_ids % NT == 1, max(1, NB // 2), live_count)
    filled = jnp.arange(NB, dtype=jnp.int32)[None, :] < live_count[:, None]
    return jnp.where(filled, chosen, -1).astype(jnp.int32)


def pairing(key):
    folded = jax.random.fold_in(key, 7)
    first_key, second_key, third_key = jax.random.split(folded, 3)
    replica_ids = jnp.arange(REPS, dtype=jnp.int32)
    anchor = jax.random.randint(first_key, (), 0, REPS)
    scores = jax.random.randint(second_key, (REPS,), 0, 65536) * REPS + replica_ids
    scores = jnp.where(replica_ids == anchor, -2, scores)
    scores = jnp.where(replica_ids == (anchor + REPS // 2) % REPS, -1, scores)
    ordering = jnp.argsort(scores).astype(jnp.int32)
    cut = jax.random.randint(third_key, (), min(3, REPS - 1), REPS)
    rest = jnp.maximum(REPS - cut, 1)
    following = jnp.where(replica_ids < cut, (replica_ids + 1) % cut, cut + (replica_ids - cut + 1) % rest)
    mates = jnp.zeros((REPS,), jnp.int32).at[ordering].set(ordering[following])
    accepted = jnp.zeros((REPS,), jnp.int32).at[ordering].set((replica_ids < cut).astype(jnp.int32))
    return (mates.astype(jnp.int32), accepted.astype(jnp.int32))


def draw_partner(key, part):
    return pairing(key)[0]


def draw_decision(key, part):
    return pairing(key)[1]


def shard_levels(key, shape, shards, smallest, top_value):
    gain, own = 1.0, jax.random.fold_in(key, 6)
    for dim, blocks in shards:
        steps = jnp.exp(jax.random.uniform(jax.random.fold_in(own, dim), (blocks,), jnp.float32, smallest / len(shards), top_value / len(shards)))
        gain = gain * jnp.repeat(steps, shape[dim] // blocks).reshape([-1 if axis == dim else 1 for axis in range(len(shape))])
    return gain


def routed_block(own_key, own, number, rows, amount, top, limit, skew):
    sequence = jax.random.permutation(own_key, amount)
    packed, ordinary = portions_of(amount, rows * top, limit, skew, True), portions_of(amount, rows * top, limit, skew, False)
    places = jnp.arange(amount)

    def named(tallies, offset_by):
        used = int((tallies > 0).sum())
        fixed = max(1, used // 4)
        moved = fixed + (places - fixed + offset_by * (used - fixed)) % max(1, amount - fixed)
        return jnp.zeros((amount,), jnp.int32).at[sequence[jnp.where(places < fixed, places, moved)]].set(jnp.asarray(tallies, jnp.int32))

    tallies = jnp.where(number % 4 == 0, named(packed, number // 4), named(ordinary, number - number // 4 - 1))
    mixed = jax.random.permutation(jax.random.fold_in(own, 3), amount)
    source_of, taker = mixed[0:amount // 2 * 2:2], mixed[1:amount // 2 * 2:2]
    margin = jnp.minimum(tallies[source_of] - 1, limit - tallies[taker]) // 2
    margin = jnp.where((source_of == sequence[0]) | (taker == sequence[0]) | (tallies[taker] == 0), 0, jnp.maximum(margin, 0))
    moved = jax.random.randint(jax.random.fold_in(own, 4), (amount // 2,), 0, 1 << 20) % (margin + 1)
    tallies = tallies.at[source_of].add(-moved).at[taker].add(moved)
    labels = jnp.searchsorted(jnp.cumsum(tallies), jnp.arange(rows * top), side="right").astype(jnp.int32)
    table = labels.reshape(top, rows).T
    table = table[jax.random.permutation(jax.random.fold_in(own, 1), rows)]
    offset_by = jax.random.randint(jax.random.fold_in(own, 2), (rows, 1), 0, top)
    return jnp.take_along_axis(table, (jnp.arange(top)[None, :] + offset_by) % top, axis=1)


def portions_of(number_of, total, reach, lean, full):
    weights = [(1 << 20) // math.isqrt(rank ** lean) + 1 for rank in range(1, number_of + 1)]
    largest = reach if full else min(reach, max(-(-total // number_of), total * weights[0] // sum(weights)))
    least = 1 if total - largest >= number_of - 1 else 0
    given, spare = [largest] + [least] * (number_of - 1), total - largest - least * (number_of - 1)
    while spare > 0:
        free = [i for i in range(1, number_of) if given[i] < largest] or [i for i in range(1, number_of) if given[i] < reach]
        mass, left = sum([weights[i] for i in free]), spare
        for i in free:
            extra = min(reach - given[i], max(1, left * weights[i] // mass), spare)
            given[i] = given[i] + extra
            spare = spare - extra
    return np.array(given)


def noise(rng, shape, deviation, bound, shards=(), kind=jnp.bfloat16):
    values = jax.random.normal(rng, shape, jnp.float32) * deviation
    if len(shards) > 0:
        values = shard_levels(rng, shape, shards, -0.22, 0.18) * values
    return jnp.clip(values, min=-bound, max=bound).astype(kind)


def setup_inputs(seed: int = 0) -> dict:
    key_list = jax.random.split(jax.random.key(seed), 14)
    positions = noise(key_list[0], (REPS, 3, ATOMS), 1.0, 6.0, ((0, 16), (2, 32)), jnp.float32)
    velocities = noise(key_list[1], (REPS, 3, ATOMS), 1.0, 6.0, ((0, 16), (2, 32)), jnp.float32)
    charge = jnp.clip(jnp.exp(math.log(2.0) - 1.3862944 * jax.random.uniform(key_list[2], (ATOMS,), jnp.float32) ** shard_levels(key_list[2], (ATOMS,), ((0, 32),), -0.2, 0.2)), 0.5, 2.0)
    inverse_mass = jnp.clip(jnp.exp(math.log(2.0) - 1.3862944 * jax.random.uniform(key_list[3], (ATOMS,), jnp.float32) ** shard_levels(key_list[3], (ATOMS,), ((0, 32),), -0.2, 0.2)), 0.5, 2.0)
    pair_tiles = draw_pair_tiles(jax.random.fold_in(key_list[13], 71), 0)
    halo_tiles = draw_halo_tiles(jax.random.fold_in(key_list[13], 71), 0)
    owners_keys = jax.random.split(jax.random.fold_in(key_list[6], 1), (DOMS * NT) // NT)
    owners_turns = jax.random.permutation(jax.random.fold_in(key_list[6], 3), (DOMS * NT) // NT)
    owners = jax.vmap(lambda own, number: routed_block(jax.random.fold_in(key_list[6], 2), own, number, NT, DOMS, OWN, CAP, 2))(owners_keys, owners_turns).reshape((DOMS * NT, OWN))
    centres = noise(key_list[7], (3, COMPS), 1.0, 6.0, ((1, 32),), jnp.float32)
    widths = jnp.clip(jnp.exp(math.log(4.0) - 1.3862944 * jax.random.uniform(key_list[8], (COMPS,), jnp.float32) ** shard_levels(key_list[8], (COMPS,), ((0, 32),), -0.2, 0.2)), 1.0, 4.0)
    map_density = jnp.clip(0.1 + 0.5 * jax.random.uniform(key_list[9], (COMPS,), jnp.float32) ** shard_levels(key_list[9], (COMPS,), ((0, 32),), -0.2, 0.2), 0.1, 0.6)
    map_error = jnp.clip(jnp.exp(math.log(0.3) - 1.0986123 * jax.random.uniform(key_list[10], (COMPS,), jnp.float32) ** shard_levels(key_list[10], (COMPS,), ((0, 32),), -0.2, 0.2)), 0.1, 0.3)
    partner = draw_partner(jax.random.fold_in(key_list[13], 71), 0)
    decision = draw_decision(jax.random.fold_in(key_list[13], 71), 0)
    return {"positions": positions, "velocities": velocities, "charge": charge, "inverse_mass": inverse_mass, "pair_tiles": pair_tiles, "halo_tiles": halo_tiles, "owners": owners, "centres": centres, "widths": widths, "map_density": map_density, "map_error": map_error, "partner": partner, "decision": decision}


highest = lax.Precision.HIGHEST
time_step = 0.5
pair_width = 1.0
map_scale = 2.0


def pair_force(own_tiles, neighbours, pair_gain):
    squared = jnp.zeros(neighbours.shape[:2] + (own_tiles.shape[2], neighbours.shape[3]), jnp.float32)
    for dim_index in range(3):
        apart = own_tiles[:, None, dim_index, :, None] - neighbours[:, :, dim_index, None, :]
        squared = squared + apart * apart
    weights = jnp.exp(-squared / (2.0 * pair_width)) * neighbours[:, :, 3, None, :]
    weight_sum = jnp.sum(weights, (1, 3))
    pulled = jnp.einsum('bjat,bjct->bca', weights, neighbours[:, :, :3, :], precision=highest)
    return (pair_gain / pair_width) * own_tiles[:, 3, None, :] * (own_tiles[:, :3, :] * weight_sum[:, None, :] - pulled)


def tile_gaussians(coords, centre, extent):
    squared = jnp.zeros((coords.shape[0], centre.shape[1], coords.shape[2], centre.shape[3]), jnp.float32)
    for dim_index in range(3):
        apart = coords[:, None, dim_index, :, None] - centre[:, :, dim_index, None, :]
        squared = squared + apart * apart
    return jnp.exp(-squared / (2.0 * extent[:, :, None, :]))


def neighbour_ids(pair_tiles, halo_tiles):
    domain_ids = jnp.arange(DOMS * NT, dtype=jnp.int32) // NT
    lower_dom = (domain_ids - 1) % DOMS
    upper_dom = (domain_ids + 1) % DOMS
    entries = pair_tiles
    local_ids = domain_ids[:, None] * NT + entries
    lower_list = halo_tiles[lower_dom][:, 1, :]
    upper_list = halo_tiles[upper_dom][:, 0, :]
    lower_index = jnp.clip(entries - NT, 0, HALO_T - 1).astype(jnp.int32)
    upper_index = jnp.clip(entries - NT - HALO_T, 0, HALO_T - 1).astype(jnp.int32)
    from_lower = lower_dom[:, None] * NT + jnp.take_along_axis(lower_list, lower_index, 1)
    from_upper = upper_dom[:, None] * NT + jnp.take_along_axis(upper_list, upper_index, 1)
    global_ids = jnp.where(entries < NT, local_ids, jnp.where(entries < NT + HALO_T, from_lower, from_upper))
    return jnp.where(entries < 0, -1, global_ids).astype(jnp.int32)


def reference(positions, velocities, charge, inverse_mass, pair_tiles, halo_tiles, owners, centres, widths, map_density, map_error, partner, decision):
    tile_count = DOMS * NT
    tile_ids = neighbour_ids(pair_tiles, halo_tiles)
    valid_mask = (tile_ids >= 0).astype(jnp.float32)
    safe_ids = jnp.maximum(tile_ids, 0)
    charges = charge.reshape(tile_count, TILE)
    inverse = inverse_mass.reshape(tile_count, TILE)
    centre_table = centres.reshape(3, DOMS, COMP_DEV).transpose(1, 0, 2)
    width_table = widths.reshape(DOMS, COMP_DEV)
    density_table = map_density.reshape(DOMS, COMP_DEV)
    error_table = map_error.reshape(DOMS, COMP_DEV)
    chosen_centres = centre_table[owners]
    chosen_widths = width_table[owners]
    pair_gain = (NB * TILE) ** -0.5
    intersection_scale = 1.0 / (OWN * NT * TILE)
    map_gain = map_scale / (OWN * COMP_DEV)
    blocks = tile_count // 8

    def blocked(array):
        return array.reshape((blocks, 8) + array.shape[1:])

    def nonbonded(coords):
        stacked = jnp.concatenate([coords, charges[:, None, :]], 1)
        near_tiles = stacked[safe_ids] * valid_mask[:, :, None, None]

        def one_block(pieces):
            return pair_force(pieces[0], pieces[1], pair_gain)

        return lax.map(one_block, (blocked(stacked), blocked(near_tiles))).reshape(tile_count, 3, TILE)

    def intersections(coords):
        def one_block(pieces):
            return jnp.sum(tile_gaussians(pieces[0], pieces[1], pieces[2]), 2) * intersection_scale

        partial_value = lax.map(one_block, (blocked(coords), blocked(chosen_centres), blocked(chosen_widths)))
        return jax.ops.segment_sum(partial_value.reshape(tile_count * OWN, COMP_DEV), owners.reshape(-1), DOMS)

    def map_forces(coords, coefficient):
        chosen_coef = coefficient[owners]

        def one_block(pieces):
            weighted = tile_gaussians(pieces[0], pieces[1], pieces[2]) * pieces[3][:, :, None, :]
            row_sum = jnp.sum(weighted, (1, 3))
            pulled = jnp.einsum('bjak,bjck->bca', weighted, pieces[1], precision=highest)
            return pieces[0] * row_sum[:, None, :] - pulled

        return lax.map(one_block, (blocked(coords), blocked(chosen_centres), blocked(chosen_widths), blocked(chosen_coef))).reshape(tile_count, 3, TILE)

    position = positions.reshape(REPS, 3, tile_count, TILE).transpose(0, 2, 1, 3)
    velocity = velocities.reshape(REPS, 3, tile_count, TILE).transpose(0, 2, 1, 3)
    model_map = jnp.zeros((DOMS, COMP_DEV), jnp.float32)
    for step_index in range(STEPS):
        summed = jnp.sum(lax.map(intersections, position), 0)
        model_map = summed / REPS
        coefficient = map_gain * (model_map - density_table) / (error_table * error_table) / width_table

        def replica_forces(coords):
            return nonbonded(coords) + map_forces(coords, coefficient)

        forces = lax.map(replica_forces, position)
        velocity = velocity + time_step * inverse[None, :, None, :] * forces
        position = position + time_step * velocity
    source = jnp.where(decision == 1, partner, jnp.arange(REPS, dtype=jnp.int32))
    position = position[source].transpose(0, 2, 1, 3).reshape(REPS, 3, tile_count * TILE)
    velocity = velocity[source].transpose(0, 2, 1, 3).reshape(REPS, 3, tile_count * TILE)
    return position, velocity, model_map.reshape(-1)
```

```python
import functools
import math

import jax
import jax.numpy as jnp
from jax import lax
from jax.experimental import pallas as pl
from jax.experimental.pallas import tpu as pltpu
from jax.sharding import PartitionSpec as P

STEPS = 2
TIME_STEP = 0.5
MAP_SCALE = 2.0
LOG2E = 1.4426950408889634
F32 = jnp.float32
BF16 = jnp.bfloat16
MESH = pl.DeviceIdType.MESH
NN = (((1,), (0,)), ((), ()))
NT = (((1,), (1,)), ((), ()))
LANES = 128
GROUPS = 8


def dot(a, b, dims):
    return lax.dot_general(a, b, dims, preferred_element_type=F32)


def split3(v):
    h = v.astype(BF16).astype(F32)
    rest = v - h
    m = rest.astype(BF16).astype(F32)
    return h, m, rest - m


def kernel(
    reps, doms, near, owned,
    pos, vel, charge, imass, pair, halo, owners, inv, cen, wid, den, err, partner, decision,
    opos, ovel, omap,
    row, out2, col, own, hs, hr, raw, pa, cf, ad, bf, qf, scr, scr2, at, pb, pq, fp, g2, part,
    d1, r1, t1, r2, cs, co, ms, mm,
    sem_px, sem_py, sem_a, sem_ad, sem_b, sem_c, sem_h, sem_hs, sem_1, sem_2, sem_3, sem_m,
):
    width = math.isqrt(reps)
    height = reps // width
    levels = doms // 2
    classes = reps // 4
    held = levels // classes
    tiles = 8
    slots = tiles * owned
    plane = 2 * reps

    r = lax.axis_index("rep")
    dom = lax.axis_index("dom")
    z = lax.div(dom, 2)
    c = lax.rem(dom, 2)
    y = lax.div(r, width)
    x = lax.rem(r, width)
    p = 2 * r + c
    below = lax.rem(dom + doms - 1, doms)
    above = lax.rem(dom + 1, doms)

    def plane_peer(i):
        k = lax.rem(p + i, plane)
        return k, (lax.div(k, 2), 2 * z + lax.rem(k, 2))

    def level_peer(i):
        return (r, 2 * lax.rem(z + i, levels) + c)

    def rep_peer(i):
        return (lax.rem(r + i, reps), dom)

    other_core = (r, 2 * z + 1 - c)

    def send(src, dst, sems, to):
        pltpu.make_async_remote_copy(
            src_ref=src, dst_ref=dst, send_sem=sems.at[0], recv_sem=sems.at[1],
            device_id=to, device_id_type=MESH,
        ).start()

    def each(count, body):
        def step(i, carry):
            body(i)
            return carry

        lax.fori_loop(1, count, step, 0)

    def received(ref, sems):
        pltpu.make_async_copy(ref, ref, sems.at[1]).wait()

    def sent(ref, sems):
        pltpu.make_async_copy(ref, ref, sems.at[0]).wait()

    barrier = pltpu.get_barrier_semaphore()

    def greet(to):
        pl.semaphore_signal(barrier, inc=1, device_id=to, device_id_type=MESH)

    each(plane, lambda i: greet(plane_peer(i)[1]))
    each(levels, lambda i: greet(level_peer(i)))
    greet((r, jnp.where(c == 0, below, above)))

    for t in range(tiles):
        for k in range(3):
            cut = slice(t * LANES, (t + 1) * LANES)
            row[x, k, t : t + 1, :] = pos[0, k : k + 1, cut]
            row[x, 3 + k, t : t + 1, :] = vel[0, k : k + 1, cut]
    for k in range(3):
        for g in range(GROUPS):
            raw[k, g : g + 1, :] = cen[k : k + 1, g * LANES : (g + 1) * LANES]
    raw[3] = wid[...]
    scr[...] = jnp.zeros_like(scr)
    scr2[...] = jnp.zeros_like(scr2)
    part[slots] = jnp.zeros((GROUPS, LANES), F32)

    pl.semaphore_wait(barrier, plane - 1 + levels - 1 + 1)

    each(width, lambda i: send(row.at[x], row.at[x], sem_px, (y * width + lax.rem(x + i, width), dom)))

    feature = lax.rem(r, 4)
    sender = lax.rem(z, classes) == lax.div(r, 4)
    place = lax.div(z, classes)

    @pl.when(sender)
    def _():
        each(levels, lambda i: send(raw.at[feature], pa.at[place], sem_a, level_peer(i)))
        pa[place] = raw[feature]

    @pl.when(z == r)
    def _():
        error = err[...]
        ad[0] = (MAP_SCALE / (owned * GROUPS * LANES)) / (error * error) / wid[...]
        ad[1] = den[...]
        each(levels, lambda i: send(ad, ad, sem_ad, level_peer(i)))

    if held > 1:
        @pl.when(sender)
        def _():
            received(pa.at[pl.ds(0, held - 1)], sem_a)

    @pl.when(jnp.logical_not(sender))
    def _():
        received(pa, sem_a)

    each(reps, lambda i: send(pa, cf.at[c, r], sem_b, rep_peer(i)))
    cf[c, r] = pa[...]

    def source_of(k):
        return jnp.where(decision[k] == 1, partner[k], k)

    received(row.at[pl.ds(0, width - 1)], sem_px)
    for i in range(1, height):
        there = lax.rem(y + i, height)
        to = there * width + x
        out2[i - 1] = row[lax.rem(source_of(to), width)]
        send(out2.at[i - 1], col.at[y], sem_py, (to, dom))
    mine = source_of(r)
    col[y] = row[lax.rem(mine, width)]
    received(col.at[pl.ds(0, height - 1)], sem_py)
    state = col[lax.div(mine, width)]
    for t in range(tiles):
        for k in range(3):
            own[t, k : k + 1, :] = state[k, t : t + 1, :]
            own[t, 4 + k : 5 + k, :] = state[3 + k, t : t + 1, :]
        own[t, 3:4, :] = charge[t : t + 1, :]
        own[t, 7:8, :] = imass[t : t + 1, :]

    def send_halo(s):
        for side, to in ((0, below), (1, above)):
            for i in range(2):
                hs[s, side, i] = own[halo[0, side, i]]
            pltpu.make_async_remote_copy(
                src_ref=hs.at[s, side], dst_ref=hr.at[s, 1 - side],
                send_sem=sem_hs.at[s, side], recv_sem=sem_h.at[s, side],
                device_id=(r, to), device_id_type=MESH,
            ).start()

    def wait_halo(s):
        for side in range(2):
            pltpu.make_async_copy(hr.at[s, 1 - side], hr.at[s, 1 - side], sem_h.at[s, side]).wait()

    send_halo(0)

    def basis(zz, cc):
        cut = lax.div(zz, classes)
        base = lax.rem(zz, classes) * 4
        cx, cy, cz, w = (cf[cc, base + f, cut] for f in range(4))
        return cx, cy, cz, w

    def component_features(cc):
        def step(zz, carry):
            cx, cy, cz, w = basis(zz, cc)
            iw = LOG2E / w
            half = -0.5 * iw
            terms = [split3(v) for v in (cx * iw, cy * iw, cz * iw, half)]
            for group, level in enumerate((0, 1, 0, 2, 0, 1)):
                for f in range(4):
                    scr[pl.ds(group * 4 + f, GROUPS, stride=32), :] = terms[f][level]
            for level, v in enumerate(split3(half * (cx * cx + cy * cy + cz * cz))):
                scr[pl.ds(24 + level, GROUPS, stride=32), :] = v
            o = 2 * zz + cc
            for g in range(GROUPS):
                bf[o, :, g * LANES : (g + 1) * LANES] = scr[g * 32 : (g + 1) * 32, :].astype(BF16)
            return carry

        lax.fori_loop(0, levels, step, 0)

    def coefficient_features(s):
        def one(zz, cc):
            cx, cy, cz, _ = basis(zz, cc)
            o = 2 * zz + cc
            coef = co[s, o]
            for f, v in enumerate((coef, coef * cx, coef * cy, coef * cz)):
                for level, piece in enumerate(split3(v)):
                    scr2[pl.ds(level * 4 + f, GROUPS, stride=16), :] = piece
            for g in range(GROUPS):
                qf[o, :, g * LANES : (g + 1) * LANES] = scr2[g * 16 : (g + 1) * 16, :].astype(BF16)

        def step(zz, carry):
            one(zz, 0)
            one(zz, 1)
            return carry

        lax.fori_loop(0, levels, step, 0)

    ones3 = jnp.ones((3, LANES), F32)
    zeros4 = jnp.zeros((4, LANES), F32)
    zeros5 = jnp.zeros((5, LANES), F32)

    def atom_features():
        for t in range(tiles):
            xyz = own[t, 0:3, :]
            h, m, l = split3(jnp.concatenate([xyz, jnp.sum(xyz * xyz, 0, keepdims=True)], 0))
            rows = jnp.concatenate([h, h, m, h, l, m, ones3, zeros5], 0)
            at[t] = rows.T.astype(BF16)

    def pair_features(s):
        for i in range(tiles + 4):
            tile = own[i] if i < tiles else hr[s, (i - tiles) // 2, (i - tiles) % 2]
            xyz = tile[0:3]
            h, m, l = split3(jnp.concatenate([xyz * LOG2E, jnp.full((1, LANES), -0.5 * LOG2E, F32)], 0))
            ch, cm, cl = split3((-0.5 * LOG2E) * jnp.sum(xyz * xyz, 0, keepdims=True))
            pb[i] = jnp.concatenate([h, m, h, l, h, m, ch, cm, cl, zeros5], 0).astype(BF16)
            q = tile[3:4]
            h, m, l = split3(jnp.concatenate([q, q * xyz], 0))
            pq[i] = jnp.concatenate([h, m, l, zeros4], 0).astype(BF16)
        pb[tiles + 4] = jnp.zeros((32, LANES), BF16)
        pq[tiles + 4] = jnp.zeros((16, LANES), BF16)

    def halves(g):
        h = g.astype(BF16)
        return h, (g - h.astype(F32)).astype(BF16)

    def pulled(sums, xyz):
        sums = sums[0:4] + sums[4:8] + sums[8:12]
        return xyz * sums[0:1] - sums[1:4]

    pair_gain = (near * LANES) ** -0.5

    def pair_pass():
        def step(t, carry):
            names = [pair[t, j] for j in range(near)]
            names = [jnp.where(n < 0, tiles + 4, n) for n in names]
            g = jnp.exp2(dot(at[t], jnp.concatenate([pb[n] for n in names], 1), NN))
            q = jnp.concatenate([pq[n] for n in names], 1)
            h, l = halves(g)
            sums = dot(q, h, NT) + dot(q, l, NT)
            fp[t, 0:3, :] = (pair_gain * own[t, 3:4, :]) * pulled(sums, own[t, 0:3, :])
            return carry

        lax.fori_loop(0, tiles, step, 0)

    chunk = 256

    def intersection_pass():
        def step(t, carry):
            a = at[t]
            for j in range(owned):
                o = owners[t, j]
                n = t * owned + j
                for q in range(GROUPS * LANES // chunk):
                    cut = slice(q * chunk, (q + 1) * chunk)
                    g = jnp.exp2(dot(a, bf[o, :, cut], NN))
                    total = jnp.sum(g, 0, keepdims=True)
                    for i in range(chunk // LANES):
                        k = q * (chunk // LANES) + i
                        part[n, k : k + 1, :] = total[:, i * LANES : (i + 1) * LANES]
                    h, l = halves(g)
                    g2[n, 0:LANES, cut] = h
                    g2[n, LANES : 2 * LANES, cut] = l
            return carry

        lax.fori_loop(0, tiles, step, 0)

    def force_pass():
        def step(t, carry):
            sums = jnp.zeros((16, 2 * LANES), F32)
            for j in range(owned):
                sums = sums + dot(qf[owners[t, j]], g2[t * owned + j], NT)
            sums = sums[:, :LANES] + sums[:, LANES:]
            xyz = own[t, 0:3, :]
            force = fp[t, 0:3, :] + pulled(sums, xyz)
            v = own[t, 4:7, :] + TIME_STEP * own[t, 7:8, :] * force
            own[t, 4:7, :] = v
            own[t, 0:3, :] = xyz + TIME_STEP * v
            return carry

        lax.fori_loop(0, tiles, step, 0)

    received(cf.at[c, pl.ds(0, reps - 1)], sem_b)
    send(cf.at[c], cf.at[c], sem_c, other_core)
    atom_features()
    component_features(c)
    received(cf.at[1 - c], sem_c)
    component_features(1 - c)

    @pl.when(z != r)
    def _():
        received(ad, sem_ad)

    for s in range(STEPS):
        if s > 0:
            send_halo(s)
            atom_features()
        intersection_pass()

        def gather(k, carry, s=s):
            d1[s, k] = part[inv[0, k]] + part[inv[1, k]]
            return carry

        lax.fori_loop(0, plane, gather, 0)

        def scatter(i, s=s):
            k, to = plane_peer(i)
            send(d1.at[s, k], r1.at[s, p], sem_1.at[s], to)

        each(plane, scatter)
        r1[s, p] = d1[s, p]

        wait_halo(s)
        pair_features(s)
        pair_pass()

        received(r1.at[s, pl.ds(0, plane - 1)], sem_1.at[s])
        total = jnp.sum(r1[s], 0)
        t1[s] = total
        each(levels, lambda i, s=s: send(t1.at[s], r2.at[s, z], sem_2.at[s], level_peer(i)))
        r2[s, z] = total
        received(r2.at[s, pl.ds(0, levels - 1)], sem_2.at[s])
        mean = jnp.sum(r2[s], 0) * (1.0 / (owned * tiles * LANES * reps))
        coef = ad[0] * (mean - ad[1])
        cs[s] = coef
        each(plane, lambda i, s=s: send(cs.at[s], co.at[s, p], sem_3.at[s], plane_peer(i)[1]))
        co[s, p] = coef
        if s == STEPS - 1:
            @pl.when(z == r)
            def _(mean=mean):
                ms[...] = mean
                omap[...] = mean
                each(reps, lambda i: send(ms, mm, sem_m, rep_peer(i)))

        received(co.at[s, pl.ds(0, plane - 1)], sem_3.at[s])
        coefficient_features(s)
        force_pass()

    for t in range(tiles):
        cut = slice(t * LANES, (t + 1) * LANES)
        opos[0, :, cut] = own[t, 0:3, :]
        ovel[0, :, cut] = own[t, 4:7, :]

    @pl.when(z != r)
    def _():
        received(mm, sem_m)
        omap[...] = mm[...]

    sent(row.at[pl.ds(0, width - 1)], sem_px)
    sent(out2, sem_py)

    @pl.when(sender)
    def _():
        sent(r2.at[0, pl.ds(0, levels - 1)], sem_a)

    @pl.when(z == r)
    def _():
        sent(d1.at[0, pl.ds(0, 2 * (levels - 1))], sem_ad)
        sent(d1.at[0, pl.ds(0, reps - 1)], sem_m)

    sent(cf.at[0, pl.ds(0, reps - 1)], sem_b)
    sent(cf.at[0], sem_c)
    for s in range(STEPS):
        for side in range(2):
            pltpu.make_async_copy(hs.at[s, side], hs.at[s, side], sem_hs.at[s, side]).wait()
        sent(d1.at[s, pl.ds(0, plane - 1)], sem_1.at[s])
        sent(r2.at[s, pl.ds(0, levels - 1)], sem_2.at[s])
        sent(co.at[s, pl.ds(0, plane - 1)], sem_3.at[s])


def local(
    positions, velocities, charge, inverse_mass, pair_tiles, halo_tiles, owners,
    centres, widths, map_density, map_error, partner, decision,
):
    reps = lax.axis_size("rep")
    doms = lax.axis_size("dom")
    tiles, near = pair_tiles.shape
    owned = owners.shape[1]
    slots = tiles * owned
    levels = doms // 2
    width = math.isqrt(reps)
    height = reps // width
    held = levels // (reps // 4)
    plane = 2 * reps

    named = owners.reshape(1, slots) == jnp.arange(doms, dtype=jnp.int32)[:, None]
    ids = jnp.arange(slots, dtype=jnp.int32)[None, :]
    first = jnp.min(jnp.where(named, ids, slots), 1)
    last = jnp.max(jnp.where(named, ids, -1), 1)
    inv = jnp.stack([first, jnp.where(last > first, last, slots)])

    def square(v):
        return v.reshape(GROUPS, LANES)

    tile = (GROUPS, LANES)
    vmem = pl.BlockSpec(memory_space=pltpu.VMEM)
    smem = pl.BlockSpec(memory_space=pltpu.SMEM)
    pair_sems = pltpu.SemaphoreType.DMA((2,))
    step_sems = pltpu.SemaphoreType.DMA((STEPS, 2))
    outs = pl.pallas_call(
        functools.partial(kernel, reps, doms, near, owned),
        out_shape=[
            jax.ShapeDtypeStruct(positions.shape, F32),
            jax.ShapeDtypeStruct(velocities.shape, F32),
            jax.ShapeDtypeStruct(tile, F32),
        ],
        in_specs=[vmem] * 4 + [smem] * 4 + [vmem] * 4 + [smem] * 2,
        out_specs=[vmem] * 3,
        scratch_shapes=[
            pltpu.VMEM((width, 6) + tile, F32),
            pltpu.VMEM((height - 1, 6) + tile, F32),
            pltpu.VMEM((height, 6) + tile, F32),
            pltpu.VMEM((tiles,) + tile, F32),
            pltpu.VMEM((STEPS, 2, 2) + tile, F32),
            pltpu.VMEM((STEPS, 2, 2) + tile, F32),
            pltpu.VMEM((4,) + tile, F32),
            pltpu.VMEM((held,) + tile, F32),
            pltpu.VMEM((2, reps, held) + tile, F32),
            pltpu.VMEM((2,) + tile, F32),
            pltpu.VMEM((doms, 32, GROUPS * LANES), BF16),
            pltpu.VMEM((doms, 16, GROUPS * LANES), BF16),
            pltpu.VMEM((GROUPS * 32, LANES), F32),
            pltpu.VMEM((GROUPS * 16, LANES), F32),
            pltpu.VMEM((tiles, LANES, 32), BF16),
            pltpu.VMEM((tiles + 5, 32, LANES), BF16),
            pltpu.VMEM((tiles + 5, 16, LANES), BF16),
            pltpu.VMEM((tiles,) + tile, F32),
            pltpu.VMEM((slots, 2 * LANES, GROUPS * LANES), BF16),
            pltpu.VMEM((slots + 1,) + tile, F32),
            pltpu.VMEM((STEPS, plane) + tile, F32),
            pltpu.VMEM((STEPS, plane) + tile, F32),
            pltpu.VMEM((STEPS,) + tile, F32),
            pltpu.VMEM((STEPS, levels) + tile, F32),
            pltpu.VMEM((STEPS,) + tile, F32),
            pltpu.VMEM((STEPS, plane) + tile, F32),
            pltpu.VMEM(tile, F32),
            pltpu.VMEM(tile, F32),
            pair_sems, pair_sems, pair_sems, pair_sems, pair_sems, pair_sems,
            step_sems, step_sems, step_sems, step_sems, step_sems,
            pair_sems,
        ],
        compiler_params=pltpu.CompilerParams(
            collective_id=0, has_side_effects=True, vmem_limit_bytes=44 * 1024 * 1024
        ),
    )(
        positions, velocities, square(charge), square(inverse_mass), pair_tiles, halo_tiles, owners,
        inv, centres, square(widths), square(map_density), square(map_error), partner, decision,
    )
    return outs[0], outs[1], outs[2].reshape(GROUPS * LANES)


def solution(mesh):
    placed = (
        P("rep", None, "dom"),
        P("rep", None, "dom"),
        P("dom"),
        P("dom"),
        P("dom", None),
        P("dom", None, None),
        P("dom", None),
        P(None, "dom"),
        P("dom"),
        P("dom"),
        P("dom"),
        P(),
        P(),
    )
    return jax.shard_map(
        local,
        mesh=mesh,
        in_specs=placed,
        out_specs=(P("rep", None, "dom"), P("rep", None, "dom"), P("dom")),
        check_vma=False,
    )
```

```python
import functools
import math

import jax
import jax.numpy as jnp
from jax import lax
from jax.experimental import pallas as pl
from jax.experimental.pallas import tpu as pltpu
from jax.sharding import PartitionSpec as P

STEPS = 2
TIME_STEP = 0.5
MAP_SCALE = 2.0
LOG2E = 1.4426950408889634
F32 = jnp.float32
BF16 = jnp.bfloat16
MESH = pl.DeviceIdType.MESH
NN = (((1,), (0,)), ((), ()))
NT = (((1,), (1,)), ((), ()))
LANES = 128
GROUPS = 8


def dot(a, b, dims):
    return lax.dot_general(a, b, dims, preferred_element_type=F32)


def split3(v):
    h = v.astype(BF16).astype(F32)
    rest = v - h
    m = rest.astype(BF16).astype(F32)
    return h, m, rest - m


def kernel(
    reps, doms, near, owned,
    pos, vel, charge, imass, pair, halo, owners, inv, cen, wid, den, err, partner, decision,
    opos, ovel, omap,
    row, out2, col, own, hs, hr, raw, pa, cf, ad, bf, bt, qf, scr, scr2, at, ar, pb, pq, fp, g2, part,
    d1, r1, t1, r2, cs, co, ms, mm,
    sem_px, sem_py, sem_a, sem_ad, sem_b, sem_c, sem_h, sem_hs, sem_1, sem_2, sem_3, sem_m,
):
    width = math.isqrt(reps)
    height = reps // width
    levels = doms // 2
    classes = reps // 4
    held = levels // classes
    tiles = 8
    slots = tiles * owned
    plane = 2 * reps

    r = lax.axis_index("rep")
    dom = lax.axis_index("dom")
    z = lax.div(dom, 2)
    c = lax.rem(dom, 2)
    y = lax.div(r, width)
    x = lax.rem(r, width)
    p = 2 * r + c
    below = lax.rem(dom + doms - 1, doms)
    above = lax.rem(dom + 1, doms)

    def around(i, count):
        return min(i, count - i)

    def wrap(v, count):
        return jnp.where(v >= count, v - count, v)

    offsets = [(i, j, k) for i in range(height) for j in range(width) for k in range(2)]
    offsets.sort(key=lambda o: -(around(o[0], height) + around(o[1], width) + 0.1 * o[2]))
    plane_offsets = offsets[:-1]
    rep_offsets = [o for o in plane_offsets if o[2] == 0]
    level_offsets = sorted(range(1, levels), key=lambda i: -around(i, levels))

    def plane_peer(o):
        there = wrap(y + o[0], height) * width + wrap(x + o[1], width)
        core = 1 - c if o[2] else c
        return 2 * there + core, (there, 2 * z + core)

    def level_peer(i):
        return (r, 2 * wrap(z + i, levels) + c)

    other_core = (r, 2 * z + 1 - c)

    def send(src, dst, sems, to):
        pltpu.make_async_remote_copy(
            src_ref=src, dst_ref=dst, send_sem=sems.at[0], recv_sem=sems.at[1],
            device_id=to, device_id_type=MESH,
        ).start()

    def received(ref, sems):
        pltpu.make_async_copy(ref, ref, sems.at[1]).wait()

    def sent(ref, sems):
        pltpu.make_async_copy(ref, ref, sems.at[0]).wait()

    barrier = pltpu.get_barrier_semaphore()

    def greet(to):
        pl.semaphore_signal(barrier, inc=1, device_id=to, device_id_type=MESH)

    for i in level_offsets:
        greet(level_peer(i))
    for o in plane_offsets:
        greet(plane_peer(o)[1])
    greet((r, jnp.where(c == 0, below, above)))

    row[x, 0:3] = pos[...]
    row[x, 3:6] = vel[...]
    for k in range(3):
        for g in range(GROUPS):
            raw[k, g : g + 1, :] = cen[k : k + 1, g * LANES : (g + 1) * LANES]
    raw[3] = wid[...]
    scr[...] = jnp.zeros_like(scr)
    scr2[...] = jnp.zeros_like(scr2)
    part[slots] = jnp.zeros((GROUPS, LANES), F32)

    pl.semaphore_wait(barrier, plane - 1 + levels - 1 + 1)

    feature = lax.rem(r, 4)
    sender = lax.rem(z, classes) == lax.div(r, 4)
    place = lax.div(z, classes)

    @pl.when(sender)
    def _():
        for i in level_offsets:
            send(raw.at[feature], pa.at[place], sem_a, level_peer(i))
        pa[place] = raw[feature]

    for i in range(1, width):
        send(row.at[x], row.at[x], sem_px, (y * width + wrap(x + i, width), dom))

    @pl.when(z == r)
    def _():
        error = err[...]
        ad[0] = (MAP_SCALE / (owned * GROUPS * LANES)) / (error * error) / wid[...]
        ad[1] = den[...]
        for i in level_offsets:
            send(ad, ad, sem_ad, level_peer(i))

    if held > 1:
        @pl.when(sender)
        def _():
            received(pa.at[pl.ds(0, held - 1)], sem_a)

    @pl.when(jnp.logical_not(sender))
    def _():
        received(pa, sem_a)

    for o in rep_offsets:
        send(pa, cf.at[c, r], sem_b, plane_peer(o)[1])
    cf[c, r] = pa[...]

    def source_of(k):
        return jnp.where(decision[k] == 1, partner[k], k)

    received(row.at[pl.ds(0, width - 1)], sem_px)
    for i in range(1, height):
        there = wrap(y + i, height)
        to = there * width + x
        out2[i - 1] = row[lax.rem(source_of(to), width)]
        send(out2.at[i - 1], col.at[y], sem_py, (to, dom))
    mine = source_of(r)
    col[y] = row[lax.rem(mine, width)]
    received(col.at[pl.ds(0, height - 1)], sem_py)
    state = col[lax.div(mine, width)]
    for t in range(tiles):
        for k in range(3):
            own[t, k : k + 1, :] = state[k, t : t + 1, :]
            own[t, 4 + k : 5 + k, :] = state[3 + k, t : t + 1, :]
        own[t, 3:4, :] = charge[t : t + 1, :]
        own[t, 7:8, :] = imass[t : t + 1, :]

    def send_halo(s):
        for side, to in ((0, below), (1, above)):
            for i in range(2):
                hs[s, side, i] = own[halo[0, side, i]]
            pltpu.make_async_remote_copy(
                src_ref=hs.at[s, side], dst_ref=hr.at[s, 1 - side],
                send_sem=sem_hs.at[s, side], recv_sem=sem_h.at[s, side],
                device_id=(r, to), device_id_type=MESH,
            ).start()

    def wait_halo(s):
        for side in range(2):
            pltpu.make_async_copy(hr.at[s, 1 - side], hr.at[s, 1 - side], sem_h.at[s, side]).wait()

    send_halo(0)

    def basis(zz, cc):
        cut = lax.div(zz, classes)
        base = lax.rem(zz, classes) * 4
        cx, cy, cz, w = (cf[cc, base + f, cut] for f in range(4))
        return cx, cy, cz, w

    def component_features(cc):
        def step(zz, carry):
            cx, cy, cz, w = basis(zz, cc)
            iw = LOG2E / w
            half = -0.5 * iw
            terms = [split3(v) for v in (cx * iw, cy * iw, cz * iw, half)]
            for group, level in enumerate((0, 1, 0, 2, 0, 1)):
                for f in range(4):
                    scr[pl.ds(group * 4 + f, GROUPS, stride=32), :] = terms[f][level]
            for level, v in enumerate(split3(half * (cx * cx + cy * cy + cz * cz))):
                scr[pl.ds(24 + level, GROUPS, stride=32), :] = v
            o = 2 * zz + cc
            for g in range(GROUPS):
                bf[o, :, g * LANES : (g + 1) * LANES] = scr[g * 32 : (g + 1) * 32, :].astype(BF16)
            return carry

        lax.fori_loop(0, levels, step, 0)

    def coefficient_features(s):
        def one(zz, cc):
            cx, cy, cz, _ = basis(zz, cc)
            o = 2 * zz + cc
            coef = co[s, o]
            for f, v in enumerate((coef, coef * cx, coef * cy, coef * cz)):
                for level, piece in enumerate(split3(v)):
                    scr2[pl.ds(level * 4 + f, GROUPS, stride=16), :] = piece
            for g in range(GROUPS):
                qf[o, :, g * LANES : (g + 1) * LANES] = scr2[g * 16 : (g + 1) * 16, :].astype(BF16)

        def step(zz, carry):
            one(zz, 0)
            one(zz, 1)
            return carry

        lax.fori_loop(0, levels, step, 0)

    ones3 = jnp.ones((3, LANES), F32)
    zeros4 = jnp.zeros((4, LANES), F32)
    zeros5 = jnp.zeros((5, LANES), F32)

    def atom_features():
        for t in range(tiles):
            xyz = own[t, 0:3, :]
            h, m, l = split3(jnp.concatenate([xyz, jnp.sum(xyz * xyz, 0, keepdims=True)], 0))
            rows = jnp.concatenate([h, h, m, h, l, m, ones3, zeros5], 0)
            at[t] = rows.T.astype(BF16)
            ar[t] = rows.astype(BF16)

    def pair_features(s):
        for i in range(tiles + 4):
            tile = own[i] if i < tiles else hr[s, (i - tiles) // 2, (i - tiles) % 2]
            xyz = tile[0:3]
            h, m, l = split3(jnp.concatenate([xyz * LOG2E, jnp.full((1, LANES), -0.5 * LOG2E, F32)], 0))
            ch, cm, cl = split3((-0.5 * LOG2E) * jnp.sum(xyz * xyz, 0, keepdims=True))
            pb[i] = jnp.concatenate([h, m, h, l, h, m, ch, cm, cl, zeros5], 0).astype(BF16)
            q = tile[3:4]
            h, m, l = split3(jnp.concatenate([q, q * xyz], 0))
            pq[i] = jnp.concatenate([h, m, l, zeros4], 0).astype(BF16)
        pb[tiles + 4] = jnp.zeros((32, LANES), BF16)
        pq[tiles + 4] = jnp.zeros((16, LANES), BF16)

    def halves(g):
        h = g.astype(BF16)
        return h, (g - h.astype(F32)).astype(BF16)

    def pulled(sums, xyz):
        sums = sums[0:4] + sums[4:8] + sums[8:12]
        return xyz * sums[0:1] - sums[1:4]

    pair_gain = (near * LANES) ** -0.5

    def pair_pass():
        def step(t, carry):
            names = [pair[t, j] for j in range(near)]
            names = [jnp.where(n < 0, tiles + 4, n) for n in names]
            g = jnp.exp2(dot(at[t], jnp.concatenate([pb[n] for n in names], 1), NN))
            q = jnp.concatenate([pq[n] for n in names], 1)
            h, l = halves(g)
            sums = dot(q, h, NT) + dot(q, l, NT)
            fp[t, 0:3, :] = (pair_gain * own[t, 3:4, :]) * pulled(sums, own[t, 0:3, :])
            return carry

        lax.fori_loop(0, tiles, step, 0)

    chunk = 256

    def intersection_pass():
        def step(t, carry):
            a = at[t]
            for j in range(owned):
                o = owners[t, j]
                n = t * owned + j
                for q in range(GROUPS * LANES // chunk):
                    cut = slice(q * chunk, (q + 1) * chunk)
                    total = jnp.sum(jnp.exp2(dot(a, bf[o, :, cut], NN)), 0, keepdims=True)
                    for i in range(chunk // LANES):
                        k = q * (chunk // LANES) + i
                        part[n, k : k + 1, :] = total[:, i * LANES : (i + 1) * LANES]
            return carry

        lax.fori_loop(0, tiles, step, 0)

    def turn_features():
        def step(o, carry):
            for g in range(GROUPS):
                cut = slice(g * LANES, (g + 1) * LANES)
                bt[o, cut, :] = bf[o, :, cut].astype(F32).T.astype(BF16)
            return carry

        lax.fori_loop(0, doms, step, 0)

    def gaussian_pass(first, last):
        def step(t, carry):
            a = ar[t]
            for j in range(owned):
                o = owners[t, j]
                n = t * owned + j
                for q in range(GROUPS * LANES // chunk):
                    cut = slice(q * chunk, (q + 1) * chunk)
                    h, l = halves(jnp.exp2(dot(bt[o, cut, :], a, NN)))
                    g2[n, cut, 0:LANES] = h
                    g2[n, cut, LANES : 2 * LANES] = l
            return carry

        lax.fori_loop(first, last, step, 0)

    def force_pass():
        def step(t, carry):
            sums = jnp.zeros((16, 2 * LANES), F32)
            for j in range(owned):
                sums = sums + dot(qf[owners[t, j]], g2[t * owned + j], NN)
            sums = sums[:, :LANES] + sums[:, LANES:]
            xyz = own[t, 0:3, :]
            force = fp[t, 0:3, :] + pulled(sums, xyz)
            v = own[t, 4:7, :] + TIME_STEP * own[t, 7:8, :] * force
            own[t, 4:7, :] = v
            own[t, 0:3, :] = xyz + TIME_STEP * v
            return carry

        lax.fori_loop(0, tiles, step, 0)

    received(cf.at[c, pl.ds(0, reps - 1)], sem_b)
    send(cf.at[c], cf.at[c], sem_c, other_core)
    atom_features()
    component_features(c)
    received(cf.at[1 - c], sem_c)
    component_features(1 - c)

    @pl.when(z != r)
    def _():
        received(ad, sem_ad)

    for s in range(STEPS):
        if s > 0:
            send_halo(s)
            atom_features()
        intersection_pass()

        def gather(k, carry, s=s):
            d1[s, k] = part[inv[0, k]] + part[inv[1, k]]
            return carry

        lax.fori_loop(0, plane, gather, 0)

        for o in plane_offsets:
            k, to = plane_peer(o)
            send(d1.at[s, k], r1.at[s, p], sem_1.at[s], to)
        r1[s, p] = d1[s, p]

        wait_halo(s)
        pair_features(s)
        pair_pass()
        if s == 0:
            turn_features()

        received(r1.at[s, pl.ds(0, plane - 1)], sem_1.at[s])
        total = jnp.sum(r1[s], 0)
        t1[s] = total
        for i in level_offsets:
            send(t1.at[s], r2.at[s, z], sem_2.at[s], level_peer(i))
        r2[s, z] = total
        gaussian_pass(0, tiles)
        received(r2.at[s, pl.ds(0, levels - 1)], sem_2.at[s])
        mean = jnp.sum(r2[s], 0) * (1.0 / (owned * tiles * LANES * reps))
        coef = ad[0] * (mean - ad[1])
        cs[s] = coef
        for o in plane_offsets:
            send(cs.at[s], co.at[s, p], sem_3.at[s], plane_peer(o)[1])
        co[s, p] = coef
        if s == STEPS - 1:
            @pl.when(z == r)
            def _(mean=mean):
                ms[...] = mean
                omap[...] = mean
                for o in rep_offsets:
                    send(ms, mm, sem_m, plane_peer(o)[1])

        received(co.at[s, pl.ds(0, plane - 1)], sem_3.at[s])
        coefficient_features(s)
        force_pass()

    for t in range(tiles):
        for k in range(3):
            opos[k, t : t + 1, :] = own[t, k : k + 1, :]
            ovel[k, t : t + 1, :] = own[t, 4 + k : 5 + k, :]

    @pl.when(z != r)
    def _():
        received(mm, sem_m)
        omap[...] = mm[...]

    sent(row.at[pl.ds(0, width - 1)], sem_px)
    sent(out2, sem_py)

    @pl.when(sender)
    def _():
        sent(r2.at[0, pl.ds(0, levels - 1)], sem_a)

    @pl.when(z == r)
    def _():
        sent(d1.at[0, pl.ds(0, 2 * (levels - 1))], sem_ad)
        sent(d1.at[0, pl.ds(0, reps - 1)], sem_m)

    sent(cf.at[0, pl.ds(0, reps - 1)], sem_b)
    sent(cf.at[0], sem_c)
    for s in range(STEPS):
        for side in range(2):
            pltpu.make_async_copy(hs.at[s, side], hs.at[s, side], sem_hs.at[s, side]).wait()
        sent(d1.at[s, pl.ds(0, plane - 1)], sem_1.at[s])
        sent(r2.at[s, pl.ds(0, levels - 1)], sem_2.at[s])
        sent(co.at[s, pl.ds(0, plane - 1)], sem_3.at[s])


def local(
    positions, velocities, charge, inverse_mass, pair_tiles, halo_tiles, owners,
    centres, widths, map_density, map_error, partner, decision,
):
    reps = lax.axis_size("rep")
    doms = lax.axis_size("dom")
    tiles, near = pair_tiles.shape
    owned = owners.shape[1]
    slots = tiles * owned
    levels = doms // 2
    width = math.isqrt(reps)
    height = reps // width
    held = levels // (reps // 4)
    plane = 2 * reps

    named = owners.reshape(1, slots) == jnp.arange(doms, dtype=jnp.int32)[:, None]
    ids = jnp.arange(slots, dtype=jnp.int32)[None, :]
    first = jnp.min(jnp.where(named, ids, slots), 1)
    last = jnp.max(jnp.where(named, ids, -1), 1)
    inv = jnp.stack([first, jnp.where(last > first, last, slots)])

    def square(v):
        return v.reshape(GROUPS, LANES)

    tile = (GROUPS, LANES)
    vmem = pl.BlockSpec(memory_space=pltpu.VMEM)
    smem = pl.BlockSpec(memory_space=pltpu.SMEM)
    pair_sems = pltpu.SemaphoreType.DMA((2,))
    step_sems = pltpu.SemaphoreType.DMA((STEPS, 2))
    outs = pl.pallas_call(
        functools.partial(kernel, reps, doms, near, owned),
        out_shape=[
            jax.ShapeDtypeStruct((3,) + tile, F32),
            jax.ShapeDtypeStruct((3,) + tile, F32),
            jax.ShapeDtypeStruct(tile, F32),
        ],
        in_specs=[vmem] * 4 + [smem] * 4 + [vmem] * 4 + [smem] * 2,
        out_specs=[vmem] * 3,
        scratch_shapes=[
            pltpu.VMEM((width, 6) + tile, F32),
            pltpu.VMEM((height - 1, 6) + tile, F32),
            pltpu.VMEM((height, 6) + tile, F32),
            pltpu.VMEM((tiles,) + tile, F32),
            pltpu.VMEM((STEPS, 2, 2) + tile, F32),
            pltpu.VMEM((STEPS, 2, 2) + tile, F32),
            pltpu.VMEM((4,) + tile, F32),
            pltpu.VMEM((held,) + tile, F32),
            pltpu.VMEM((2, reps, held) + tile, F32),
            pltpu.VMEM((2,) + tile, F32),
            pltpu.VMEM((doms, 32, GROUPS * LANES), BF16),
            pltpu.VMEM((doms, GROUPS * LANES, 32), BF16),
            pltpu.VMEM((doms, 16, GROUPS * LANES), BF16),
            pltpu.VMEM((GROUPS * 32, LANES), F32),
            pltpu.VMEM((GROUPS * 16, LANES), F32),
            pltpu.VMEM((tiles, LANES, 32), BF16),
            pltpu.VMEM((tiles, 32, LANES), BF16),
            pltpu.VMEM((tiles + 5, 32, LANES), BF16),
            pltpu.VMEM((tiles + 5, 16, LANES), BF16),
            pltpu.VMEM((tiles,) + tile, F32),
            pltpu.VMEM((slots, GROUPS * LANES, 2 * LANES), BF16),
            pltpu.VMEM((slots + 1,) + tile, F32),
            pltpu.VMEM((STEPS, plane) + tile, F32),
            pltpu.VMEM((STEPS, plane) + tile, F32),
            pltpu.VMEM((STEPS,) + tile, F32),
            pltpu.VMEM((STEPS, levels) + tile, F32),
            pltpu.VMEM((STEPS,) + tile, F32),
            pltpu.VMEM((STEPS, plane) + tile, F32),
            pltpu.VMEM(tile, F32),
            pltpu.VMEM(tile, F32),
            pair_sems, pair_sems, pair_sems, pair_sems, pair_sems, pair_sems,
            step_sems, step_sems, step_sems, step_sems, step_sems,
            pair_sems,
        ],
        compiler_params=pltpu.CompilerParams(
            collective_id=0, has_side_effects=True, vmem_limit_bytes=52 * 1024 * 1024
        ),
    )(
        positions.reshape((3,) + tile), velocities.reshape((3,) + tile), square(charge), square(inverse_mass), pair_tiles, halo_tiles, owners,
        inv, centres, square(widths), square(map_density), square(map_error), partner, decision,
    )
    return outs[0].reshape(positions.shape), outs[1].reshape(velocities.shape), outs[2].reshape(GROUPS * LANES)


def solution(mesh):
    placed = (
        P("rep", None, "dom"),
        P("rep", None, "dom"),
        P("dom"),
        P("dom"),
        P("dom", None),
        P("dom", None, None),
        P("dom", None),
        P(None, "dom"),
        P("dom"),
        P("dom"),
        P("dom"),
        P(),
        P(),
    )
    return jax.shard_map(
        local,
        mesh=mesh,
        in_specs=placed,
        out_specs=(P("rep", None, "dom"), P("rep", None, "dom"), P("dom")),
        check_vma=False,
    )
```

```python
import functools
import math

import jax
import jax.numpy as jnp
from jax import lax
from jax.experimental import pallas as pl
from jax.experimental.pallas import tpu as pltpu
from jax.sharding import PartitionSpec as P

STEPS = 2
TIME_STEP = 0.5
MAP_SCALE = 2.0
LOG2E = 1.4426950408889634
F32 = jnp.float32
BF16 = jnp.bfloat16
MESH = pl.DeviceIdType.MESH
NN = (((1,), (0,)), ((), ()))
NT = (((1,), (1,)), ((), ()))
LANES = 128
GROUPS = 8


def dot(a, b, dims):
    return lax.dot_general(a, b, dims, preferred_element_type=F32)


def split3(v):
    h = v.astype(BF16).astype(F32)
    rest = v - h
    m = rest.astype(BF16).astype(F32)
    return h, m, rest - m


def kernel(
    reps, doms, near, owned,
    pos, vel, charge, imass, pair, halo, owners, inv, cen, wid, den, err, partner, decision,
    opos, ovel, omap,
    row, out2, col, own, hs, hr, raw, pa, cf, ad, bf, bt, qf, scr, scr2, at, ar, pb, pq, fp, g2, part,
    d1, r1, t1, r2, cs, co, ms, mm,
    sem_px, sem_py, sem_a, sem_ad, sem_b, sem_c, sem_h, sem_hs, sem_1, sem_2, sem_3, sem_m,
):
    width = math.isqrt(reps)
    height = reps // width
    levels = doms // 2
    classes = reps // 4
    held = levels // classes
    tiles = 8
    slots = tiles * owned
    plane = 2 * reps

    r = lax.axis_index("rep")
    dom = lax.axis_index("dom")
    z = lax.div(dom, 2)
    c = lax.rem(dom, 2)
    y = lax.div(r, width)
    x = lax.rem(r, width)
    p = 2 * r + c
    below = lax.rem(dom + doms - 1, doms)
    above = lax.rem(dom + 1, doms)

    def around(i, count):
        return min(i, count - i)

    def wrap(v, count):
        return jnp.where(v >= count, v - count, v)

    offsets = [(i, j, k) for i in range(height) for j in range(width) for k in range(2)]
    offsets.sort(key=lambda o: -(around(o[0], height) + around(o[1], width) + 0.1 * o[2]))
    plane_offsets = offsets[:-1]
    rep_offsets = [o for o in plane_offsets if o[2] == 0]
    level_offsets = sorted(range(1, levels), key=lambda i: -around(i, levels))

    def plane_peer(o):
        there = wrap(y + o[0], height) * width + wrap(x + o[1], width)
        core = 1 - c if o[2] else c
        return 2 * there + core, (there, 2 * z + core)

    def level_peer(i):
        return (r, 2 * wrap(z + i, levels) + c)

    other_core = (r, 2 * z + 1 - c)

    def send(src, dst, sems, to):
        pltpu.make_async_remote_copy(
            src_ref=src, dst_ref=dst, send_sem=sems.at[0], recv_sem=sems.at[1],
            device_id=to, device_id_type=MESH,
        ).start()

    def received(ref, sems):
        pltpu.make_async_copy(ref, ref, sems.at[1]).wait()

    def sent(ref, sems):
        pltpu.make_async_copy(ref, ref, sems.at[0]).wait()

    barrier = pltpu.get_barrier_semaphore()

    def greet(to):
        pl.semaphore_signal(barrier, inc=1, device_id=to, device_id_type=MESH)

    for i in level_offsets:
        greet(level_peer(i))
    for o in plane_offsets:
        greet(plane_peer(o)[1])
    greet((r, jnp.where(c == 0, below, above)))

    row[x, 0:3] = pos[...]
    row[x, 3:6] = vel[...]
    for k in range(3):
        for g in range(GROUPS):
            raw[k, g : g + 1, :] = cen[k : k + 1, g * LANES : (g + 1) * LANES]
    raw[3] = wid[...]
    scr[...] = jnp.zeros_like(scr)
    scr2[...] = jnp.zeros_like(scr2)
    part[slots] = jnp.zeros((GROUPS, LANES), F32)

    pl.semaphore_wait(barrier, plane - 1 + levels - 1 + 1)

    feature = lax.rem(r, 4)
    sender = lax.rem(z, classes) == lax.div(r, 4)
    place = lax.div(z, classes)

    @pl.when(sender)
    def _():
        for i in level_offsets:
            send(raw.at[feature], pa.at[place], sem_a, level_peer(i))
        pa[place] = raw[feature]

    for i in range(1, width):
        send(row.at[x], row.at[x], sem_px, (y * width + wrap(x + i, width), dom))

    @pl.when(z == r)
    def _():
        error = err[...]
        ad[0] = (MAP_SCALE / (owned * GROUPS * LANES)) / (error * error) / wid[...]
        ad[1] = den[...]
        for i in level_offsets:
            send(ad, ad, sem_ad, level_peer(i))

    if held > 1:
        @pl.when(sender)
        def _():
            received(pa.at[pl.ds(0, held - 1)], sem_a)

    @pl.when(jnp.logical_not(sender))
    def _():
        received(pa, sem_a)

    for o in rep_offsets:
        send(pa, cf.at[c, r], sem_b, plane_peer(o)[1])
    cf[c, r] = pa[...]

    def source_of(k):
        return jnp.where(decision[k] == 1, partner[k], k)

    received(row.at[pl.ds(0, width - 1)], sem_px)
    for i in range(1, height):
        there = wrap(y + i, height)
        to = there * width + x
        out2[i - 1] = row[lax.rem(source_of(to), width)]
        send(out2.at[i - 1], col.at[y], sem_py, (to, dom))
    mine = source_of(r)
    col[y] = row[lax.rem(mine, width)]
    received(col.at[pl.ds(0, height - 1)], sem_py)
    state = col[lax.div(mine, width)]
    for t in range(tiles):
        for k in range(3):
            own[t, k : k + 1, :] = state[k, t : t + 1, :]
            own[t, 4 + k : 5 + k, :] = state[3 + k, t : t + 1, :]
        own[t, 3:4, :] = charge[t : t + 1, :]
        own[t, 7:8, :] = imass[t : t + 1, :]

    def send_halo(s):
        for side, to in ((0, below), (1, above)):
            for i in range(2):
                hs[s, side, i] = own[halo[0, side, i]]
            pltpu.make_async_remote_copy(
                src_ref=hs.at[s, side], dst_ref=hr.at[s, 1 - side],
                send_sem=sem_hs.at[s, side], recv_sem=sem_h.at[s, side],
                device_id=(r, to), device_id_type=MESH,
            ).start()

    def wait_halo(s):
        for side in range(2):
            pltpu.make_async_copy(hr.at[s, 1 - side], hr.at[s, 1 - side], sem_h.at[s, side]).wait()

    send_halo(0)

    def basis(zz, cc):
        cut = lax.div(zz, classes)
        base = lax.rem(zz, classes) * 4
        cx, cy, cz, w = (cf[cc, base + f, cut] for f in range(4))
        return cx, cy, cz, w

    def component_features(cc):
        def one(zz, u):
            cx, cy, cz, w = basis(zz, cc)
            iw = LOG2E / w
            half = -0.5 * iw
            terms = [split3(v) for v in (cx * iw, cy * iw, cz * iw, half)]
            for group, level in enumerate((0, 1, 0, 2, 0, 1)):
                for f in range(4):
                    scr[u, pl.ds(group * 4 + f, GROUPS, stride=32), :] = terms[f][level]
            for level, v in enumerate(split3(half * (cx * cx + cy * cy + cz * cz))):
                scr[u, pl.ds(24 + level, GROUPS, stride=32), :] = v

        def step(i, carry):
            for u in range(2):
                one(2 * i + u, u)
            for u in range(2):
                o = 2 * (2 * i + u) + cc
                for g in range(GROUPS):
                    bf[o, :, g * LANES : (g + 1) * LANES] = scr[u, g * 32 : (g + 1) * 32, :].astype(BF16)
            return carry

        lax.fori_loop(0, levels // 2, step, 0)

    def coefficient_features(s):
        def one(zz, cc, u):
            cx, cy, cz, _ = basis(zz, cc)
            coef = co[s, 2 * zz + cc]
            for f, v in enumerate((coef, coef * cx, coef * cy, coef * cz)):
                for level, piece in enumerate(split3(v)):
                    scr2[u, pl.ds(level * 4 + f, GROUPS, stride=16), :] = piece

        def step(i, carry):
            for u in range(4):
                one(2 * i + u // 2, u % 2, u)
            for u in range(4):
                for g in range(GROUPS):
                    qf[4 * i + u, :, g * LANES : (g + 1) * LANES] = scr2[u, g * 16 : (g + 1) * 16, :].astype(BF16)
            return carry

        lax.fori_loop(0, doms // 4, step, 0)

    ones3 = jnp.ones((3, LANES), F32)
    zeros4 = jnp.zeros((4, LANES), F32)
    zeros5 = jnp.zeros((5, LANES), F32)

    def atom_features():
        for t in range(tiles):
            xyz = own[t, 0:3, :]
            h, m, l = split3(jnp.concatenate([xyz, jnp.sum(xyz * xyz, 0, keepdims=True)], 0))
            rows = jnp.concatenate([h, h, m, h, l, m, ones3, zeros5], 0)
            at[t] = rows.T.astype(BF16)
            ar[t] = rows.astype(BF16)

    def pair_features(s):
        for i in range(tiles + 4):
            tile = own[i] if i < tiles else hr[s, (i - tiles) // 2, (i - tiles) % 2]
            xyz = tile[0:3]
            h, m, l = split3(jnp.concatenate([xyz * LOG2E, jnp.full((1, LANES), -0.5 * LOG2E, F32)], 0))
            ch, cm, cl = split3((-0.5 * LOG2E) * jnp.sum(xyz * xyz, 0, keepdims=True))
            pb[i] = jnp.concatenate([h, m, h, l, h, m, ch, cm, cl, zeros5], 0).astype(BF16)
            q = tile[3:4]
            h, m, l = split3(jnp.concatenate([q, q * xyz], 0))
            pq[i] = jnp.concatenate([h, m, l, zeros4], 0).astype(BF16)
        pb[tiles + 4] = jnp.zeros((32, LANES), BF16)
        pq[tiles + 4] = jnp.zeros((16, LANES), BF16)

    def halves(g):
        h = g.astype(BF16)
        return h, (g - h.astype(F32)).astype(BF16)

    def pulled(sums, xyz):
        sums = sums[0:4] + sums[4:8] + sums[8:12]
        return xyz * sums[0:1] - sums[1:4]

    pair_gain = (near * LANES) ** -0.5

    def pair_pass():
        def step(t, carry):
            names = [pair[t, j] for j in range(near)]
            names = [jnp.where(n < 0, tiles + 4, n) for n in names]
            g = jnp.exp2(dot(at[t], jnp.concatenate([pb[n] for n in names], 1), NN))
            q = jnp.concatenate([pq[n] for n in names], 1)
            h, l = halves(g)
            sums = dot(q, h, NT) + dot(q, l, NT)
            fp[t, 0:3, :] = (pair_gain * own[t, 3:4, :]) * pulled(sums, own[t, 0:3, :])
            return carry

        lax.fori_loop(0, tiles, step, 0)

    chunk = 256

    def intersection_pass():
        def one(t):
            a = at[t]
            for j in range(owned):
                o = owners[t, j]
                n = t * owned + j
                for q in range(GROUPS * LANES // chunk):
                    cut = slice(q * chunk, (q + 1) * chunk)
                    total = jnp.sum(jnp.exp2(dot(a, bf[o, :, cut], NN)), 0, keepdims=True)
                    for i in range(chunk // LANES):
                        k = q * (chunk // LANES) + i
                        part[n, k : k + 1, :] = total[:, i * LANES : (i + 1) * LANES]

        def step(i, carry):
            one(2 * i)
            one(2 * i + 1)
            return carry

        lax.fori_loop(0, tiles // 2, step, 0)

    def turn_features():
        def step(o, carry):
            for g in range(GROUPS):
                cut = slice(g * LANES, (g + 1) * LANES)
                bt[o, cut, :] = bf[o, :, cut].astype(F32).T.astype(BF16)
            return carry

        lax.fori_loop(0, doms, step, 0)

    def gaussian_pass(first, last):
        def step(t, carry):
            a = ar[t]
            for j in range(owned):
                o = owners[t, j]
                n = t * owned + j
                for q in range(GROUPS * LANES // chunk):
                    cut = slice(q * chunk, (q + 1) * chunk)
                    h, l = halves(jnp.exp2(dot(bt[o, cut, :], a, NN)))
                    g2[n, cut, 0:LANES] = h
                    g2[n, cut, LANES : 2 * LANES] = l
            return carry

        lax.fori_loop(first, last, step, 0)

    def force_pass():
        def one(t):
            sums = jnp.zeros((16, 2 * LANES), F32)
            for j in range(owned):
                sums = sums + dot(qf[owners[t, j]], g2[t * owned + j], NN)
            sums = sums[:, :LANES] + sums[:, LANES:]
            xyz = own[t, 0:3, :]
            force = fp[t, 0:3, :] + pulled(sums, xyz)
            v = own[t, 4:7, :] + TIME_STEP * own[t, 7:8, :] * force
            own[t, 4:7, :] = v
            own[t, 0:3, :] = xyz + TIME_STEP * v

        def step(i, carry):
            one(2 * i)
            one(2 * i + 1)
            return carry

        lax.fori_loop(0, tiles // 2, step, 0)

    received(cf.at[c, pl.ds(0, reps - 1)], sem_b)
    send(cf.at[c], cf.at[c], sem_c, other_core)
    atom_features()
    component_features(c)
    received(cf.at[1 - c], sem_c)
    component_features(1 - c)

    @pl.when(z != r)
    def _():
        received(ad, sem_ad)

    for s in range(STEPS):
        if s > 0:
            send_halo(s)
            atom_features()
        intersection_pass()

        for k in range(plane):
            d1[s, k] = part[inv[0, k]] + part[inv[1, k]]

        for o in plane_offsets:
            k, to = plane_peer(o)
            send(d1.at[s, k], r1.at[s, p], sem_1.at[s], to)
        r1[s, p] = d1[s, p]

        wait_halo(s)
        pair_features(s)
        pair_pass()

        received(r1.at[s, pl.ds(0, plane - 1)], sem_1.at[s])
        total = jnp.sum(r1[s], 0)
        t1[s] = total
        for i in level_offsets:
            send(t1.at[s], r2.at[s, z], sem_2.at[s], level_peer(i))
        r2[s, z] = total
        if s == 0:
            turn_features()
        early = 4 if s == 0 else 6
        gaussian_pass(0, early)
        received(r2.at[s, pl.ds(0, levels - 1)], sem_2.at[s])
        mean = jnp.sum(r2[s], 0) * (1.0 / (owned * tiles * LANES * reps))
        coef = ad[0] * (mean - ad[1])
        cs[s] = coef
        for o in plane_offsets:
            send(cs.at[s], co.at[s, p], sem_3.at[s], plane_peer(o)[1])
        co[s, p] = coef
        if s == STEPS - 1:
            @pl.when(z == r)
            def _(mean=mean):
                ms[...] = mean
                omap[...] = mean
                for o in rep_offsets:
                    send(ms, mm, sem_m, plane_peer(o)[1])

        gaussian_pass(early, tiles)
        received(co.at[s, pl.ds(0, plane - 1)], sem_3.at[s])
        coefficient_features(s)
        force_pass()

    for t in range(tiles):
        for k in range(3):
            opos[k, t : t + 1, :] = own[t, k : k + 1, :]
            ovel[k, t : t + 1, :] = own[t, 4 + k : 5 + k, :]

    @pl.when(z != r)
    def _():
        received(mm, sem_m)
        omap[...] = mm[...]

    sent(row.at[pl.ds(0, width - 1)], sem_px)
    sent(out2, sem_py)

    @pl.when(sender)
    def _():
        sent(r2.at[0, pl.ds(0, levels - 1)], sem_a)

    @pl.when(z == r)
    def _():
        sent(d1.at[0, pl.ds(0, 2 * (levels - 1))], sem_ad)
        sent(d1.at[0, pl.ds(0, reps - 1)], sem_m)

    sent(cf.at[0, pl.ds(0, reps - 1)], sem_b)
    sent(cf.at[0], sem_c)
    for s in range(STEPS):
        for side in range(2):
            pltpu.make_async_copy(hs.at[s, side], hs.at[s, side], sem_hs.at[s, side]).wait()
        sent(d1.at[s, pl.ds(0, plane - 1)], sem_1.at[s])
        sent(r2.at[s, pl.ds(0, levels - 1)], sem_2.at[s])
        sent(co.at[s, pl.ds(0, plane - 1)], sem_3.at[s])


def local(
    positions, velocities, charge, inverse_mass, pair_tiles, halo_tiles, owners,
    centres, widths, map_density, map_error, partner, decision,
):
    reps = lax.axis_size("rep")
    doms = lax.axis_size("dom")
    tiles, near = pair_tiles.shape
    owned = owners.shape[1]
    slots = tiles * owned
    levels = doms // 2
    width = math.isqrt(reps)
    height = reps // width
    held = levels // (reps // 4)
    plane = 2 * reps

    named = owners.reshape(1, slots) == jnp.arange(doms, dtype=jnp.int32)[:, None]
    ids = jnp.arange(slots, dtype=jnp.int32)[None, :]
    first = jnp.min(jnp.where(named, ids, slots), 1)
    last = jnp.max(jnp.where(named, ids, -1), 1)
    inv = jnp.stack([first, jnp.where(last > first, last, slots)])

    def square(v):
        return v.reshape(GROUPS, LANES)

    tile = (GROUPS, LANES)
    vmem = pl.BlockSpec(memory_space=pltpu.VMEM)
    smem = pl.BlockSpec(memory_space=pltpu.SMEM)
    pair_sems = pltpu.SemaphoreType.DMA((2,))
    step_sems = pltpu.SemaphoreType.DMA((STEPS, 2))
    outs = pl.pallas_call(
        functools.partial(kernel, reps, doms, near, owned),
        out_shape=[
            jax.ShapeDtypeStruct((3,) + tile, F32),
            jax.ShapeDtypeStruct((3,) + tile, F32),
            jax.ShapeDtypeStruct(tile, F32),
        ],
        in_specs=[vmem] * 4 + [smem] * 4 + [vmem] * 4 + [smem] * 2,
        out_specs=[vmem] * 3,
        scratch_shapes=[
            pltpu.VMEM((width, 6) + tile, F32),
            pltpu.VMEM((height - 1, 6) + tile, F32),
            pltpu.VMEM((height, 6) + tile, F32),
            pltpu.VMEM((tiles,) + tile, F32),
            pltpu.VMEM((STEPS, 2, 2) + tile, F32),
            pltpu.VMEM((STEPS, 2, 2) + tile, F32),
            pltpu.VMEM((4,) + tile, F32),
            pltpu.VMEM((held,) + tile, F32),
            pltpu.VMEM((2, reps, held) + tile, F32),
            pltpu.VMEM((2,) + tile, F32),
            pltpu.VMEM((doms, 32, GROUPS * LANES), BF16),
            pltpu.VMEM((doms, GROUPS * LANES, 32), BF16),
            pltpu.VMEM((doms, 16, GROUPS * LANES), BF16),
            pltpu.VMEM((2, GROUPS * 32, LANES), F32),
            pltpu.VMEM((4, GROUPS * 16, LANES), F32),
            pltpu.VMEM((tiles, LANES, 32), BF16),
            pltpu.VMEM((tiles, 32, LANES), BF16),
            pltpu.VMEM((tiles + 5, 32, LANES), BF16),
            pltpu.VMEM((tiles + 5, 16, LANES), BF16),
            pltpu.VMEM((tiles,) + tile, F32),
            pltpu.VMEM((slots, GROUPS * LANES, 2 * LANES), BF16),
            pltpu.VMEM((slots + 1,) + tile, F32),
            pltpu.VMEM((STEPS, plane) + tile, F32),
            pltpu.VMEM((STEPS, plane) + tile, F32),
            pltpu.VMEM((STEPS,) + tile, F32),
            pltpu.VMEM((STEPS, levels) + tile, F32),
            pltpu.VMEM((STEPS,) + tile, F32),
            pltpu.VMEM((STEPS, plane) + tile, F32),
            pltpu.VMEM(tile, F32),
            pltpu.VMEM(tile, F32),
            pair_sems, pair_sems, pair_sems, pair_sems, pair_sems, pair_sems,
            step_sems, step_sems, step_sems, step_sems, step_sems,
            pair_sems,
        ],
        compiler_params=pltpu.CompilerParams(
            collective_id=0, has_side_effects=True, vmem_limit_bytes=52 * 1024 * 1024
        ),
    )(
        positions.reshape((3,) + tile), velocities.reshape((3,) + tile), square(charge), square(inverse_mass), pair_tiles, halo_tiles, owners,
        inv, centres, square(widths), square(map_density), square(map_error), partner, decision,
    )
    return outs[0].reshape(positions.shape), outs[1].reshape(velocities.shape), outs[2].reshape(GROUPS * LANES)


def solution(mesh):
    placed = (
        P("rep", None, "dom"),
        P("rep", None, "dom"),
        P("dom"),
        P("dom"),
        P("dom", None),
        P("dom", None, None),
        P("dom", None),
        P(None, "dom"),
        P("dom"),
        P("dom"),
        P("dom"),
        P(),
        P(),
    )
    return jax.shard_map(
        local,
        mesh=mesh,
        in_specs=placed,
        out_specs=(P("rep", None, "dom"), P("rep", None, "dom"), P("dom")),
        check_vma=False,
    )
```

```python
import functools
import math

import jax
import jax.numpy as jnp
from jax import lax
from jax.experimental import pallas as pl
from jax.experimental.pallas import tpu as pltpu
from jax.sharding import PartitionSpec as P

STEPS = 2
TIME_STEP = 0.5
MAP_SCALE = 2.0
LOG2E = 1.4426950408889634
F32 = jnp.float32
BF16 = jnp.bfloat16
MESH = pl.DeviceIdType.MESH
NN = (((1,), (0,)), ((), ()))
NT = (((1,), (1,)), ((), ()))
LANES = 128
GROUPS = 8


def dot(a, b, dims):
    return lax.dot_general(a, b, dims, preferred_element_type=F32)


def split3(v):
    h = v.astype(BF16).astype(F32)
    rest = v - h
    m = rest.astype(BF16).astype(F32)
    return h, m, rest - m


def kernel(
    reps, doms, near, owned,
    pos, vel, charge_in, imass_in, pair, halo, owners, inv, cen_in, wid, den_in, err_in, partner, decision,
    opos, ovel, omap,
    charge, imass, cen, den, err, row, out2, col, own, hs, hr, raw, pa, cf, ad, bf, bt, qf, scr, scr2, at, ar, pb, pq, fp, g2, part,
    d1, r1, t1, r2, cs, co, ms, mm,
    sem_px, sem_py, sem_a, sem_ad, sem_b, sem_c, sem_h, sem_hs, sem_1, sem_2, sem_3, sem_m, sem_in,
):
    width = math.isqrt(reps)
    height = reps // width
    levels = doms // 2
    classes = reps // 4
    held = levels // classes
    tiles = 8
    slots = tiles * owned
    plane = 2 * reps

    r = lax.axis_index("rep")
    dom = lax.axis_index("dom")
    z = lax.div(dom, 2)
    c = lax.rem(dom, 2)
    y = lax.div(r, width)
    x = lax.rem(r, width)
    p = 2 * r + c
    below = lax.rem(dom + doms - 1, doms)
    above = lax.rem(dom + 1, doms)

    def around(i, count):
        return min(i, count - i)

    def wrap(v, count):
        return jnp.where(v >= count, v - count, v)

    offsets = [(i, j, k) for i in range(height) for j in range(width) for k in range(2)]
    offsets.sort(key=lambda o: -(around(o[0], height) + around(o[1], width) + 0.1 * o[2]))
    plane_offsets = offsets[:-1]
    rep_offsets = [o for o in plane_offsets if o[2] == 0]
    level_offsets = sorted(range(1, levels), key=lambda i: -around(i, levels))

    def plane_peer(o):
        there = wrap(y + o[0], height) * width + wrap(x + o[1], width)
        core = 1 - c if o[2] else c
        return 2 * there + core, (there, 2 * z + core)

    def level_peer(i):
        return (r, 2 * wrap(z + i, levels) + c)

    other_core = (r, 2 * z + 1 - c)

    def send(src, dst, sems, to):
        pltpu.make_async_remote_copy(
            src_ref=src, dst_ref=dst, send_sem=sems.at[0], recv_sem=sems.at[1],
            device_id=to, device_id_type=MESH,
        ).start()

    def received(ref, sems):
        pltpu.make_async_copy(ref, ref, sems.at[1]).wait()

    def sent(ref, sems):
        pltpu.make_async_copy(ref, ref, sems.at[0]).wait()

    barrier = pltpu.get_barrier_semaphore()

    def greet(to):
        pl.semaphore_signal(barrier, inc=1, device_id=to, device_id_type=MESH)

    for i in level_offsets:
        greet(level_peer(i))
    for o in plane_offsets:
        greet(plane_peer(o)[1])
    greet((r, jnp.where(c == 0, below, above)))

    wanted = (
        (cen_in, cen), (wid, raw.at[3]), (pos, row.at[x, pl.ds(0, 3)]), (vel, row.at[x, pl.ds(3, 3)]),
        (charge_in, charge), (imass_in, imass), (den_in, den), (err_in, err),
    )
    loads = [pltpu.make_async_copy(src, dst, sem_in.at[i]) for i, (src, dst) in enumerate(wanted)]
    for load in loads:
        load.start()
    scr[...] = jnp.zeros_like(scr)
    scr2[...] = jnp.zeros_like(scr2)
    part[slots] = jnp.zeros((GROUPS, LANES), F32)
    for load in loads:
        load.wait()
    for k in range(3):
        for g in range(GROUPS):
            raw[k, g : g + 1, :] = cen[k : k + 1, g * LANES : (g + 1) * LANES]

    pl.semaphore_wait(barrier, plane - 1 + levels - 1 + 1)

    feature = lax.rem(r, 4)
    sender = lax.rem(z, classes) == lax.div(r, 4)
    place = lax.div(z, classes)

    @pl.when(sender)
    def _():
        for i in level_offsets:
            send(raw.at[feature], pa.at[place], sem_a, level_peer(i))
        pa[place] = raw[feature]

    for i in range(1, width):
        send(row.at[x], row.at[x], sem_px, (y * width + wrap(x + i, width), dom))

    @pl.when(z == r)
    def _():
        error = err[...]
        ad[0] = (MAP_SCALE / (owned * GROUPS * LANES)) / (error * error) / raw[3]
        ad[1] = den[...]
        for i in level_offsets:
            send(ad, ad, sem_ad, level_peer(i))

    if held > 1:
        @pl.when(sender)
        def _():
            received(pa.at[pl.ds(0, held - 1)], sem_a)

    @pl.when(jnp.logical_not(sender))
    def _():
        received(pa, sem_a)

    for o in rep_offsets:
        send(pa, cf.at[c, r], sem_b, plane_peer(o)[1])
    cf[c, r] = pa[...]

    def source_of(k):
        return jnp.where(decision[k] == 1, partner[k], k)

    received(row.at[pl.ds(0, width - 1)], sem_px)
    for i in range(1, height):
        there = wrap(y + i, height)
        to = there * width + x
        out2[i - 1] = row[lax.rem(source_of(to), width)]
        send(out2.at[i - 1], col.at[y], sem_py, (to, dom))
    mine = source_of(r)
    col[y] = row[lax.rem(mine, width)]
    received(col.at[pl.ds(0, height - 1)], sem_py)
    state = col[lax.div(mine, width)]
    for t in range(tiles):
        for k in range(3):
            own[t, k : k + 1, :] = state[k, t : t + 1, :]
            own[t, 4 + k : 5 + k, :] = state[3 + k, t : t + 1, :]
        own[t, 3:4, :] = charge[t : t + 1, :]
        own[t, 7:8, :] = imass[t : t + 1, :]

    def send_halo(s):
        for side, to in ((0, below), (1, above)):
            for i in range(2):
                hs[s, side, i] = own[halo[0, side, i]]
            pltpu.make_async_remote_copy(
                src_ref=hs.at[s, side], dst_ref=hr.at[s, 1 - side],
                send_sem=sem_hs.at[s, side], recv_sem=sem_h.at[s, side],
                device_id=(r, to), device_id_type=MESH,
            ).start()

    def wait_halo(s):
        for side in range(2):
            pltpu.make_async_copy(hr.at[s, 1 - side], hr.at[s, 1 - side], sem_h.at[s, side]).wait()

    send_halo(0)

    def basis(zz, cc):
        cut = lax.div(zz, classes)
        base = lax.rem(zz, classes) * 4
        cx, cy, cz, w = (cf[cc, base + f, cut] for f in range(4))
        return cx, cy, cz, w

    def component_features(cc):
        def one(zz, u):
            cx, cy, cz, w = basis(zz, cc)
            iw = LOG2E / w
            half = -0.5 * iw
            terms = [split3(v) for v in (cx * iw, cy * iw, cz * iw, half)]
            for group, level in enumerate((0, 1, 0, 2, 0, 1)):
                for f in range(4):
                    scr[u, pl.ds(group * 4 + f, GROUPS, stride=32), :] = terms[f][level]
            for level, v in enumerate(split3(half * (cx * cx + cy * cy + cz * cz))):
                scr[u, pl.ds(24 + level, GROUPS, stride=32), :] = v

        def step(i, carry):
            for u in range(2):
                one(2 * i + u, u)
            for u in range(2):
                o = 2 * (2 * i + u) + cc
                for g in range(GROUPS):
                    bf[o, :, g * LANES : (g + 1) * LANES] = scr[u, g * 32 : (g + 1) * 32, :].astype(BF16)
            return carry

        lax.fori_loop(0, levels // 2, step, 0)

    def coefficient_features(s):
        def one(zz, cc, u):
            cx, cy, cz, _ = basis(zz, cc)
            coef = co[s, 2 * zz + cc]
            for f, v in enumerate((coef, coef * cx, coef * cy, coef * cz)):
                for level, piece in enumerate(split3(v)):
                    scr2[u, pl.ds(level * 4 + f, GROUPS, stride=16), :] = piece

        def step(i, carry):
            for u in range(4):
                one(2 * i + u // 2, u % 2, u)
            for u in range(4):
                for g in range(GROUPS):
                    qf[4 * i + u, :, g * LANES : (g + 1) * LANES] = scr2[u, g * 16 : (g + 1) * 16, :].astype(BF16)
            return carry

        lax.fori_loop(0, doms // 4, step, 0)

    ones3 = jnp.ones((3, LANES), F32)
    zeros4 = jnp.zeros((4, LANES), F32)
    zeros5 = jnp.zeros((5, LANES), F32)

    def atom_features():
        for t in range(tiles):
            xyz = own[t, 0:3, :]
            h, m, l = split3(jnp.concatenate([xyz, jnp.sum(xyz * xyz, 0, keepdims=True)], 0))
            rows = jnp.concatenate([h, h, m, h, l, m, ones3, zeros5], 0)
            at[t] = rows.T.astype(BF16)
            ar[t] = rows.astype(BF16)

    def pair_features(s):
        for i in range(tiles + 4):
            tile = own[i] if i < tiles else hr[s, (i - tiles) // 2, (i - tiles) % 2]
            xyz = tile[0:3]
            h, m, l = split3(jnp.concatenate([xyz * LOG2E, jnp.full((1, LANES), -0.5 * LOG2E, F32)], 0))
            ch, cm, cl = split3((-0.5 * LOG2E) * jnp.sum(xyz * xyz, 0, keepdims=True))
            pb[i] = jnp.concatenate([h, m, h, l, h, m, ch, cm, cl, zeros5], 0).astype(BF16)
            q = tile[3:4]
            h, m, l = split3(jnp.concatenate([q, q * xyz], 0))
            pq[i] = jnp.concatenate([h, m, l, zeros4], 0).astype(BF16)
        pb[tiles + 4] = jnp.zeros((32, LANES), BF16)
        pq[tiles + 4] = jnp.zeros((16, LANES), BF16)

    def halves(g):
        h = g.astype(BF16)
        return h, (g - h.astype(F32)).astype(BF16)

    def pulled(sums, xyz):
        sums = sums[0:4] + sums[4:8] + sums[8:12]
        return xyz * sums[0:1] - sums[1:4]

    pair_gain = (near * LANES) ** -0.5

    def pair_pass():
        def step(t, carry):
            names = [pair[t, j] for j in range(near)]
            names = [jnp.where(n < 0, tiles + 4, n) for n in names]
            g = jnp.exp2(dot(at[t], jnp.concatenate([pb[n] for n in names], 1), NN))
            q = jnp.concatenate([pq[n] for n in names], 1)
            h, l = halves(g)
            sums = dot(q, h, NT) + dot(q, l, NT)
            fp[t, 0:3, :] = (pair_gain * own[t, 3:4, :]) * pulled(sums, own[t, 0:3, :])
            return carry

        lax.fori_loop(0, tiles, step, 0)

    chunk = 256

    def intersection_pass():
        def one(t):
            a = at[t]
            for j in range(owned):
                o = owners[j, t]
                n = t * owned + j
                for q in range(GROUPS * LANES // chunk):
                    cut = slice(q * chunk, (q + 1) * chunk)
                    total = jnp.sum(jnp.exp2(dot(a, bf[o, :, cut], NN)), 0, keepdims=True)
                    for i in range(chunk // LANES):
                        k = q * (chunk // LANES) + i
                        part[n, k : k + 1, :] = total[:, i * LANES : (i + 1) * LANES]

        def step(i, carry):
            one(2 * i)
            one(2 * i + 1)
            return carry

        lax.fori_loop(0, tiles // 2, step, 0)

    def turn_features():
        def step(o, carry):
            for g in range(GROUPS):
                cut = slice(g * LANES, (g + 1) * LANES)
                bt[o, cut, :] = bf[o, :, cut].astype(F32).T.astype(BF16)
            return carry

        lax.fori_loop(0, doms, step, 0)

    def gaussian_pass(first, last):
        def step(t, carry):
            a = ar[t]
            for j in range(owned):
                o = owners[j, t]
                n = t * owned + j
                for q in range(GROUPS * LANES // chunk):
                    cut = slice(q * chunk, (q + 1) * chunk)
                    h, l = halves(jnp.exp2(dot(bt[o, cut, :], a, NN)))
                    g2[n, cut, 0:LANES] = h
                    g2[n, cut, LANES : 2 * LANES] = l
            return carry

        lax.fori_loop(first, last, step, 0)

    def force_pass():
        def one(t):
            sums = jnp.zeros((16, 2 * LANES), F32)
            for j in range(owned):
                sums = sums + dot(qf[owners[j, t]], g2[t * owned + j], NN)
            sums = sums[:, :LANES] + sums[:, LANES:]
            xyz = own[t, 0:3, :]
            force = fp[t, 0:3, :] + pulled(sums, xyz)
            v = own[t, 4:7, :] + TIME_STEP * own[t, 7:8, :] * force
            own[t, 4:7, :] = v
            own[t, 0:3, :] = xyz + TIME_STEP * v

        def step(i, carry):
            one(2 * i)
            one(2 * i + 1)
            return carry

        lax.fori_loop(0, tiles // 2, step, 0)

    received(cf.at[c, pl.ds(0, reps - 1)], sem_b)
    send(cf.at[c], cf.at[c], sem_c, other_core)
    atom_features()
    component_features(c)
    received(cf.at[1 - c], sem_c)
    component_features(1 - c)

    @pl.when(z != r)
    def _():
        received(ad, sem_ad)

    for s in range(STEPS):
        if s > 0:
            send_halo(s)
            atom_features()
        intersection_pass()

        for k in range(plane):
            d1[s, k] = part[inv[0, k]] + part[inv[1, k]]

        for o in plane_offsets:
            k, to = plane_peer(o)
            send(d1.at[s, k], r1.at[s, p], sem_1.at[s], to)
        r1[s, p] = d1[s, p]

        wait_halo(s)
        pair_features(s)
        pair_pass()

        received(r1.at[s, pl.ds(0, plane - 1)], sem_1.at[s])
        total = jnp.sum(r1[s], 0)
        t1[s] = total
        for i in level_offsets:
            send(t1.at[s], r2.at[s, z], sem_2.at[s], level_peer(i))
        r2[s, z] = total
        if s == 0:
            turn_features()
        early = 4 if s == 0 else 6
        gaussian_pass(0, early)
        received(r2.at[s, pl.ds(0, levels - 1)], sem_2.at[s])
        mean = jnp.sum(r2[s], 0) * (1.0 / (owned * tiles * LANES * reps))
        coef = ad[0] * (mean - ad[1])
        cs[s] = coef
        for o in plane_offsets:
            send(cs.at[s], co.at[s, p], sem_3.at[s], plane_peer(o)[1])
        co[s, p] = coef
        if s == STEPS - 1:
            @pl.when(z == r)
            def _(mean=mean):
                ms[...] = mean
                omap[...] = mean
                for o in rep_offsets:
                    send(ms, mm, sem_m, plane_peer(o)[1])

        gaussian_pass(early, tiles)
        received(co.at[s, pl.ds(0, plane - 1)], sem_3.at[s])
        coefficient_features(s)
        force_pass()

    for t in range(tiles):
        for k in range(3):
            opos[k, t : t + 1, :] = own[t, k : k + 1, :]
            ovel[k, t : t + 1, :] = own[t, 4 + k : 5 + k, :]

    @pl.when(z != r)
    def _():
        received(mm, sem_m)
        omap[...] = mm[...]

    sent(row.at[pl.ds(0, width - 1)], sem_px)
    sent(out2, sem_py)

    @pl.when(sender)
    def _():
        sent(r2.at[0, pl.ds(0, levels - 1)], sem_a)

    @pl.when(z == r)
    def _():
        sent(d1.at[0, pl.ds(0, 2 * (levels - 1))], sem_ad)
        sent(d1.at[0, pl.ds(0, reps - 1)], sem_m)

    sent(cf.at[0, pl.ds(0, reps - 1)], sem_b)
    sent(cf.at[0], sem_c)
    for s in range(STEPS):
        for side in range(2):
            pltpu.make_async_copy(hs.at[s, side], hs.at[s, side], sem_hs.at[s, side]).wait()
        sent(d1.at[s, pl.ds(0, plane - 1)], sem_1.at[s])
        sent(r2.at[s, pl.ds(0, levels - 1)], sem_2.at[s])
        sent(co.at[s, pl.ds(0, plane - 1)], sem_3.at[s])


def write_out(a, b, c, x, y, z, sems):
    moves = [pltpu.make_async_copy(u, v, sems.at[i]) for i, (u, v) in enumerate(((a, x), (b, y), (c, z)))]
    for move in moves:
        move.start()
    for move in moves:
        move.wait()


def local(
    positions, velocities, charge, inverse_mass, pair_tiles, halo_tiles, owners,
    centres, widths, map_density, map_error, partner, decision,
):
    reps = lax.axis_size("rep")
    doms = lax.axis_size("dom")
    tiles, near = pair_tiles.shape
    owned = owners.shape[1]
    slots = tiles * owned
    levels = doms // 2
    width = math.isqrt(reps)
    height = reps // width
    held = levels // (reps // 4)
    plane = 2 * reps

    turned = owners.T
    named = turned[None] == jnp.arange(doms, dtype=jnp.int32)[:, None, None]
    ids = jnp.arange(tiles, dtype=jnp.int32)[None, None, :] * owned + jnp.arange(owned, dtype=jnp.int32)[None, :, None]
    first = jnp.min(jnp.where(named, ids, slots), (1, 2))
    last = jnp.max(jnp.where(named, ids, -1), (1, 2))
    inv = jnp.stack([first, jnp.where(last > first, last, slots)])

    def square(v):
        return v.reshape(GROUPS, LANES)

    tile = (GROUPS, LANES)
    vmem = pl.BlockSpec(memory_space=pltpu.VMEM)
    hbm = pl.BlockSpec(memory_space=pltpu.HBM)
    smem = pl.BlockSpec(memory_space=pltpu.SMEM)
    pair_sems = pltpu.SemaphoreType.DMA((2,))
    step_sems = pltpu.SemaphoreType.DMA((STEPS, 2))
    outs = pl.pallas_call(
        functools.partial(kernel, reps, doms, near, owned),
        out_shape=[
            jax.ShapeDtypeStruct((3,) + tile, F32),
            jax.ShapeDtypeStruct((3,) + tile, F32),
            jax.ShapeDtypeStruct(tile, F32),
        ],
        in_specs=[hbm] * 4 + [smem] * 4 + [hbm] * 4 + [smem] * 2,
        out_specs=[vmem] * 3,
        scratch_shapes=[
            pltpu.VMEM(tile, F32),
            pltpu.VMEM(tile, F32),
            pltpu.VMEM((3, GROUPS * LANES), F32),
            pltpu.VMEM(tile, F32),
            pltpu.VMEM(tile, F32),
            pltpu.VMEM((width, 6) + tile, F32),
            pltpu.VMEM((height - 1, 6) + tile, F32),
            pltpu.VMEM((height, 6) + tile, F32),
            pltpu.VMEM((tiles,) + tile, F32),
            pltpu.VMEM((STEPS, 2, 2) + tile, F32),
            pltpu.VMEM((STEPS, 2, 2) + tile, F32),
            pltpu.VMEM((4,) + tile, F32),
            pltpu.VMEM((held,) + tile, F32),
            pltpu.VMEM((2, reps, held) + tile, F32),
            pltpu.VMEM((2,) + tile, F32),
            pltpu.VMEM((doms, 32, GROUPS * LANES), BF16),
            pltpu.VMEM((doms, GROUPS * LANES, 32), BF16),
            pltpu.VMEM((doms, 16, GROUPS * LANES), BF16),
            pltpu.VMEM((2, GROUPS * 32, LANES), F32),
            pltpu.VMEM((4, GROUPS * 16, LANES), F32),
            pltpu.VMEM((tiles, LANES, 32), BF16),
            pltpu.VMEM((tiles, 32, LANES), BF16),
            pltpu.VMEM((tiles + 5, 32, LANES), BF16),
            pltpu.VMEM((tiles + 5, 16, LANES), BF16),
            pltpu.VMEM((tiles,) + tile, F32),
            pltpu.VMEM((slots, GROUPS * LANES, 2 * LANES), BF16),
            pltpu.VMEM((slots + 1,) + tile, F32),
            pltpu.VMEM((STEPS, plane) + tile, F32),
            pltpu.VMEM((STEPS, plane) + tile, F32),
            pltpu.VMEM((STEPS,) + tile, F32),
            pltpu.VMEM((STEPS, levels) + tile, F32),
            pltpu.VMEM((STEPS,) + tile, F32),
            pltpu.VMEM((STEPS, plane) + tile, F32),
            pltpu.VMEM(tile, F32),
            pltpu.VMEM(tile, F32),
            pair_sems, pair_sems, pair_sems, pair_sems, pair_sems, pair_sems,
            step_sems, step_sems, step_sems, step_sems, step_sems,
            pair_sems,
            pltpu.SemaphoreType.DMA((8,)),
        ],
        compiler_params=pltpu.CompilerParams(
            collective_id=0, has_side_effects=True, vmem_limit_bytes=64 * 1024 * 1024
        ),
    )(
        positions.reshape((3,) + tile), velocities.reshape((3,) + tile), square(charge), square(inverse_mass), pair_tiles, halo_tiles, turned,
        inv, centres, square(widths), square(map_density), square(map_error), partner, decision,
    )
    outs = pl.pallas_call(
        write_out,
        out_shape=[jax.ShapeDtypeStruct(o.shape, F32) for o in outs],
        in_specs=[vmem] * 3,
        out_specs=[hbm] * 3,
        scratch_shapes=[pltpu.SemaphoreType.DMA((3,))],
    )(*outs)
    return outs[0].reshape(positions.shape), outs[1].reshape(velocities.shape), outs[2].reshape(GROUPS * LANES)


def solution(mesh):
    placed = (
        P("rep", None, "dom"),
        P("rep", None, "dom"),
        P("dom"),
        P("dom"),
        P("dom", None),
        P("dom", None, None),
        P("dom", None),
        P(None, "dom"),
        P("dom"),
        P("dom"),
        P("dom"),
        P(),
        P(),
    )
    return jax.shard_map(
        local,
        mesh=mesh,
        in_specs=placed,
        out_specs=(P("rep", None, "dom"), P("rep", None, "dom"), P("dom")),
        check_vma=False,
    )
```

```python
import functools
import math

import jax
import jax.numpy as jnp
from jax import lax
from jax.experimental import pallas as pl
from jax.experimental.pallas import tpu as pltpu
from jax.sharding import PartitionSpec as P

STEPS = 2
TIME_STEP = 0.5
MAP_SCALE = 2.0
LOG2E = 1.4426950408889634
F32 = jnp.float32
BF16 = jnp.bfloat16
MESH = pl.DeviceIdType.MESH
NN = (((1,), (0,)), ((), ()))
NT = (((1,), (1,)), ((), ()))
LANES = 128
GROUPS = 8


def dot(a, b, dims):
    return lax.dot_general(a, b, dims, preferred_element_type=F32)


def split3(v):
    h = v.astype(BF16).astype(F32)
    rest = v - h
    m = rest.astype(BF16).astype(F32)
    return h, m, rest - m


def kernel(
    reps, doms, near, owned,
    pos, vel, charge_in, imass_in, pair, halo, owners, cen_in, wid, den_in, err_in, partner, decision,
    opos, ovel, omap,
    inv, charge, imass, cen, den, err, row, out2, col, own, hs, hr, raw, pa, cf, ad, bf, bt, qf, scr, scr2, at, ar, pb, pq, fp, g2, part,
    d1, r1, t1, r2, cs, co, ms, mm,
    sem_px, sem_py, sem_a, sem_ad, sem_b, sem_c, sem_h, sem_hs, sem_1, sem_2, sem_3, sem_m, sem_in,
):
    width = math.isqrt(reps)
    height = reps // width
    levels = doms // 2
    classes = reps // 4
    held = levels // classes
    tiles = 8
    slots = tiles * owned
    plane = 2 * reps

    r = lax.axis_index("rep")
    dom = lax.axis_index("dom")
    z = lax.div(dom, 2)
    c = lax.rem(dom, 2)
    y = lax.div(r, width)
    x = lax.rem(r, width)
    p = 2 * r + c
    below = lax.rem(dom + doms - 1, doms)
    above = lax.rem(dom + 1, doms)

    def around(i, count):
        return min(i, count - i)

    def wrap(v, count):
        return jnp.where(v >= count, v - count, v)

    offsets = [(i, j, k) for i in range(height) for j in range(width) for k in range(2)]
    offsets.sort(key=lambda o: -(around(o[0], height) + around(o[1], width) + 0.1 * o[2]))
    plane_offsets = offsets[:-1]
    rep_offsets = [o for o in plane_offsets if o[2] == 0]
    level_offsets = sorted(range(1, levels), key=lambda i: -around(i, levels))

    def plane_peer(o):
        there = wrap(y + o[0], height) * width + wrap(x + o[1], width)
        core = 1 - c if o[2] else c
        return 2 * there + core, (there, 2 * z + core)

    def level_peer(i):
        return (r, 2 * wrap(z + i, levels) + c)

    other_core = (r, 2 * z + 1 - c)

    def send(src, dst, sems, to):
        pltpu.make_async_remote_copy(
            src_ref=src, dst_ref=dst, send_sem=sems.at[0], recv_sem=sems.at[1],
            device_id=to, device_id_type=MESH,
        ).start()

    def received(ref, sems):
        pltpu.make_async_copy(ref, ref, sems.at[1]).wait()

    def sent(ref, sems):
        pltpu.make_async_copy(ref, ref, sems.at[0]).wait()

    barrier = pltpu.get_barrier_semaphore()

    def greet(to):
        pl.semaphore_signal(barrier, inc=1, device_id=to, device_id_type=MESH)

    for i in level_offsets:
        greet(level_peer(i))
    for o in plane_offsets:
        greet(plane_peer(o)[1])
    greet((r, jnp.where(c == 0, below, above)))

    wanted = (
        (cen_in, cen), (wid, raw.at[3]), (pos, row.at[x, pl.ds(0, 3)]), (vel, row.at[x, pl.ds(3, 3)]),
        (charge_in, charge), (imass_in, imass), (den_in, den), (err_in, err),
    )
    loads = [pltpu.make_async_copy(src, dst, sem_in.at[i]) for i, (src, dst) in enumerate(wanted)]
    for load in loads:
        load.start()
    scr[...] = jnp.zeros_like(scr)
    scr2[...] = jnp.zeros_like(scr2)
    part[slots] = jnp.zeros((GROUPS, LANES), F32)

    def find(k, carry):
        one, two = slots, slots
        for t in range(tiles):
            for j in range(owned):
                hit = owners[j, t] == k
                two = jnp.where(hit, one, two)
                one = jnp.where(hit, t * owned + j, one)
        inv[0, k] = jnp.asarray(one, jnp.int32)
        inv[1, k] = jnp.asarray(two, jnp.int32)
        return carry

    lax.fori_loop(0, doms, find, 0)
    for load in loads:
        load.wait()
    for k in range(3):
        for g in range(GROUPS):
            raw[k, g : g + 1, :] = cen[k : k + 1, g * LANES : (g + 1) * LANES]

    pl.semaphore_wait(barrier, plane - 1 + levels - 1 + 1)

    feature = lax.rem(r, 4)
    sender = lax.rem(z, classes) == lax.div(r, 4)
    place = lax.div(z, classes)

    @pl.when(sender)
    def _():
        for i in level_offsets:
            send(raw.at[feature], pa.at[place], sem_a, level_peer(i))
        pa[place] = raw[feature]

    for i in range(1, width):
        send(row.at[x], row.at[x], sem_px, (y * width + wrap(x + i, width), dom))

    @pl.when(z == r)
    def _():
        error = err[...]
        ad[0] = (MAP_SCALE / (owned * GROUPS * LANES)) / (error * error) / raw[3]
        ad[1] = den[...]
        for i in level_offsets:
            send(ad, ad, sem_ad, level_peer(i))

    if held > 1:
        @pl.when(sender)
        def _():
            received(pa.at[pl.ds(0, held - 1)], sem_a)

    @pl.when(jnp.logical_not(sender))
    def _():
        received(pa, sem_a)

    for o in rep_offsets:
        send(pa, cf.at[c, r], sem_b, plane_peer(o)[1])
    cf[c, r] = pa[...]

    def source_of(k):
        return jnp.where(decision[k] == 1, partner[k], k)

    received(row.at[pl.ds(0, width - 1)], sem_px)
    for i in range(1, height):
        there = wrap(y + i, height)
        to = there * width + x
        out2[i - 1] = row[lax.rem(source_of(to), width)]
        send(out2.at[i - 1], col.at[y], sem_py, (to, dom))
    mine = source_of(r)
    col[y] = row[lax.rem(mine, width)]
    received(col.at[pl.ds(0, height - 1)], sem_py)
    state = col[lax.div(mine, width)]
    for t in range(tiles):
        for k in range(3):
            own[t, k : k + 1, :] = state[k, t : t + 1, :]
            own[t, 4 + k : 5 + k, :] = state[3 + k, t : t + 1, :]
        own[t, 3:4, :] = charge[t : t + 1, :]
        own[t, 7:8, :] = imass[t : t + 1, :]

    def send_halo(s):
        for side, to in ((0, below), (1, above)):
            for i in range(2):
                hs[s, side, i] = own[halo[0, side, i]]
            pltpu.make_async_remote_copy(
                src_ref=hs.at[s, side], dst_ref=hr.at[s, 1 - side],
                send_sem=sem_hs.at[s, side], recv_sem=sem_h.at[s, side],
                device_id=(r, to), device_id_type=MESH,
            ).start()

    def wait_halo(s):
        for side in range(2):
            pltpu.make_async_copy(hr.at[s, 1 - side], hr.at[s, 1 - side], sem_h.at[s, side]).wait()

    send_halo(0)

    def basis(zz, cc):
        cut = lax.div(zz, classes)
        base = lax.rem(zz, classes) * 4
        cx, cy, cz, w = (cf[cc, base + f, cut] for f in range(4))
        return cx, cy, cz, w

    def component_features(cc):
        def one(zz, u):
            cx, cy, cz, w = basis(zz, cc)
            iw = LOG2E / w
            half = -0.5 * iw
            terms = [split3(v) for v in (cx * iw, cy * iw, cz * iw, half)]
            for group, level in enumerate((0, 1, 0, 2, 0, 1)):
                for f in range(4):
                    scr[u, pl.ds(group * 4 + f, GROUPS, stride=32), :] = terms[f][level]
            for level, v in enumerate(split3(half * (cx * cx + cy * cy + cz * cz))):
                scr[u, pl.ds(24 + level, GROUPS, stride=32), :] = v

        def step(i, carry):
            for u in range(2):
                one(2 * i + u, u)
            for u in range(2):
                o = 2 * (2 * i + u) + cc
                for g in range(GROUPS):
                    bf[o, :, g * LANES : (g + 1) * LANES] = scr[u, g * 32 : (g + 1) * 32, :].astype(BF16)
            return carry

        lax.fori_loop(0, levels // 2, step, 0)

    def coefficient_features(s):
        def one(zz, cc, u):
            cx, cy, cz, _ = basis(zz, cc)
            coef = co[s, 2 * zz + cc]
            for f, v in enumerate((coef, coef * cx, coef * cy, coef * cz)):
                for level, piece in enumerate(split3(v)):
                    scr2[u, pl.ds(level * 4 + f, GROUPS, stride=16), :] = piece

        def step(i, carry):
            for u in range(4):
                one(2 * i + u // 2, u % 2, u)
            for u in range(4):
                for g in range(GROUPS):
                    qf[4 * i + u, :, g * LANES : (g + 1) * LANES] = scr2[u, g * 16 : (g + 1) * 16, :].astype(BF16)
            return carry

        lax.fori_loop(0, doms // 4, step, 0)

    ones3 = jnp.ones((3, LANES), F32)
    zeros4 = jnp.zeros((4, LANES), F32)
    zeros5 = jnp.zeros((5, LANES), F32)

    def atom_features():
        for t in range(tiles):
            xyz = own[t, 0:3, :]
            h, m, l = split3(jnp.concatenate([xyz, jnp.sum(xyz * xyz, 0, keepdims=True)], 0))
            rows = jnp.concatenate([h, h, m, h, l, m, ones3, zeros5], 0)
            at[t] = rows.T.astype(BF16)
            ar[t] = rows.astype(BF16)

    def pair_features(s):
        for i in range(tiles + 4):
            tile = own[i] if i < tiles else hr[s, (i - tiles) // 2, (i - tiles) % 2]
            xyz = tile[0:3]
            h, m, l = split3(jnp.concatenate([xyz * LOG2E, jnp.full((1, LANES), -0.5 * LOG2E, F32)], 0))
            ch, cm, cl = split3((-0.5 * LOG2E) * jnp.sum(xyz * xyz, 0, keepdims=True))
            pb[i] = jnp.concatenate([h, m, h, l, h, m, ch, cm, cl, zeros5], 0).astype(BF16)
            q = tile[3:4]
            h, m, l = split3(jnp.concatenate([q, q * xyz], 0))
            pq[i] = jnp.concatenate([h, m, l, zeros4], 0).astype(BF16)
        pb[tiles + 4] = jnp.zeros((32, LANES), BF16)
        pq[tiles + 4] = jnp.zeros((16, LANES), BF16)

    def halves(g):
        h = g.astype(BF16)
        return h, (g - h.astype(F32)).astype(BF16)

    def pulled(sums, xyz):
        sums = sums[0:4] + sums[4:8] + sums[8:12]
        return xyz * sums[0:1] - sums[1:4]

    pair_gain = (near * LANES) ** -0.5

    def pair_pass():
        def step(t, carry):
            names = [pair[t, j] for j in range(near)]
            names = [jnp.where(n < 0, tiles + 4, n) for n in names]
            g = jnp.exp2(dot(at[t], jnp.concatenate([pb[n] for n in names], 1), NN))
            q = jnp.concatenate([pq[n] for n in names], 1)
            h, l = halves(g)
            sums = dot(q, h, NT) + dot(q, l, NT)
            fp[t, 0:3, :] = (pair_gain * own[t, 3:4, :]) * pulled(sums, own[t, 0:3, :])
            return carry

        lax.fori_loop(0, tiles, step, 0)

    chunk = 256

    def intersection_pass():
        def one(t):
            a = at[t]
            for j in range(owned):
                o = owners[j, t]
                n = t * owned + j
                for q in range(GROUPS * LANES // chunk):
                    cut = slice(q * chunk, (q + 1) * chunk)
                    total = jnp.sum(jnp.exp2(dot(a, bf[o, :, cut], NN)), 0, keepdims=True)
                    for i in range(chunk // LANES):
                        k = q * (chunk // LANES) + i
                        part[n, k : k + 1, :] = total[:, i * LANES : (i + 1) * LANES]

        def step(i, carry):
            one(2 * i)
            one(2 * i + 1)
            return carry

        lax.fori_loop(0, tiles // 2, step, 0)

    def turn_features():
        def step(o, carry):
            for g in range(GROUPS):
                cut = slice(g * LANES, (g + 1) * LANES)
                bt[o, cut, :] = bf[o, :, cut].astype(F32).T.astype(BF16)
            return carry

        lax.fori_loop(0, doms, step, 0)

    def gaussian_pass(first, last):
        def step(t, carry):
            a = ar[t]
            for j in range(owned):
                o = owners[j, t]
                n = t * owned + j
                for q in range(GROUPS * LANES // chunk):
                    cut = slice(q * chunk, (q + 1) * chunk)
                    h, l = halves(jnp.exp2(dot(bt[o, cut, :], a, NN)))
                    g2[n, cut, 0:LANES] = h
                    g2[n, cut, LANES : 2 * LANES] = l
            return carry

        lax.fori_loop(first, last, step, 0)

    def force_pass():
        def one(t):
            sums = jnp.zeros((16, 2 * LANES), F32)
            for j in range(owned):
                sums = sums + dot(qf[owners[j, t]], g2[t * owned + j], NN)
            sums = sums[:, :LANES] + sums[:, LANES:]
            xyz = own[t, 0:3, :]
            force = fp[t, 0:3, :] + pulled(sums, xyz)
            v = own[t, 4:7, :] + TIME_STEP * own[t, 7:8, :] * force
            own[t, 4:7, :] = v
            own[t, 0:3, :] = xyz + TIME_STEP * v

        def step(i, carry):
            one(2 * i)
            one(2 * i + 1)
            return carry

        lax.fori_loop(0, tiles // 2, step, 0)

    received(cf.at[c, pl.ds(0, reps - 1)], sem_b)
    send(cf.at[c], cf.at[c], sem_c, other_core)
    atom_features()
    component_features(c)
    received(cf.at[1 - c], sem_c)
    component_features(1 - c)

    @pl.when(z != r)
    def _():
        received(ad, sem_ad)

    for s in range(STEPS):
        if s > 0:
            send_halo(s)
            atom_features()
        intersection_pass()

        for k in range(plane):
            d1[s, k] = part[inv[0, k]] + part[inv[1, k]]

        for o in plane_offsets:
            k, to = plane_peer(o)
            send(d1.at[s, k], r1.at[s, p], sem_1.at[s], to)
        r1[s, p] = d1[s, p]

        wait_halo(s)
        pair_features(s)
        pair_pass()

        received(r1.at[s, pl.ds(0, plane - 1)], sem_1.at[s])
        total = jnp.sum(r1[s], 0)
        t1[s] = total
        for i in level_offsets:
            send(t1.at[s], r2.at[s, z], sem_2.at[s], level_peer(i))
        r2[s, z] = total
        if s == 0:
            turn_features()
        early = 4 if s == 0 else 6
        gaussian_pass(0, early)
        received(r2.at[s, pl.ds(0, levels - 1)], sem_2.at[s])
        mean = jnp.sum(r2[s], 0) * (1.0 / (owned * tiles * LANES * reps))
        coef = ad[0] * (mean - ad[1])
        cs[s] = coef
        for o in plane_offsets:
            send(cs.at[s], co.at[s, p], sem_3.at[s], plane_peer(o)[1])
        co[s, p] = coef
        if s == STEPS - 1:
            @pl.when(z == r)
            def _(mean=mean):
                ms[...] = mean
                omap[...] = mean
                for o in rep_offsets:
                    send(ms, mm, sem_m, plane_peer(o)[1])

        gaussian_pass(early, tiles)
        received(co.at[s, pl.ds(0, plane - 1)], sem_3.at[s])
        coefficient_features(s)
        force_pass()

    for t in range(tiles):
        for k in range(3):
            opos[k, t : t + 1, :] = own[t, k : k + 1, :]
            ovel[k, t : t + 1, :] = own[t, 4 + k : 5 + k, :]

    @pl.when(z != r)
    def _():
        received(mm, sem_m)
        omap[...] = mm[...]

    sent(row.at[pl.ds(0, width - 1)], sem_px)
    sent(out2, sem_py)

    @pl.when(sender)
    def _():
        sent(r2.at[0, pl.ds(0, levels - 1)], sem_a)

    @pl.when(z == r)
    def _():
        sent(d1.at[0, pl.ds(0, 2 * (levels - 1))], sem_ad)
        sent(d1.at[0, pl.ds(0, reps - 1)], sem_m)

    sent(cf.at[0, pl.ds(0, reps - 1)], sem_b)
    sent(cf.at[0], sem_c)
    for s in range(STEPS):
        for side in range(2):
            pltpu.make_async_copy(hs.at[s, side], hs.at[s, side], sem_hs.at[s, side]).wait()
        sent(d1.at[s, pl.ds(0, plane - 1)], sem_1.at[s])
        sent(r2.at[s, pl.ds(0, levels - 1)], sem_2.at[s])
        sent(co.at[s, pl.ds(0, plane - 1)], sem_3.at[s])


def write_out(a, b, c, x, y, z, sems):
    moves = [pltpu.make_async_copy(u, v, sems.at[i]) for i, (u, v) in enumerate(((a, x), (b, y), (c, z)))]
    for move in moves:
        move.start()
    for move in moves:
        move.wait()


def local(
    positions, velocities, charge, inverse_mass, pair_tiles, halo_tiles, owners,
    centres, widths, map_density, map_error, partner, decision,
):
    reps = lax.axis_size("rep")
    doms = lax.axis_size("dom")
    tiles, near = pair_tiles.shape
    owned = owners.shape[1]
    slots = tiles * owned
    levels = doms // 2
    width = math.isqrt(reps)
    height = reps // width
    held = levels // (reps // 4)
    plane = 2 * reps

    def square(v):
        return v.reshape(GROUPS, LANES)

    tile = (GROUPS, LANES)
    vmem = pl.BlockSpec(memory_space=pltpu.VMEM)
    hbm = pl.BlockSpec(memory_space=pltpu.HBM)
    smem = pl.BlockSpec(memory_space=pltpu.SMEM)
    pair_sems = pltpu.SemaphoreType.DMA((2,))
    step_sems = pltpu.SemaphoreType.DMA((STEPS, 2))
    outs = pl.pallas_call(
        functools.partial(kernel, reps, doms, near, owned),
        out_shape=[
            jax.ShapeDtypeStruct((3,) + tile, F32),
            jax.ShapeDtypeStruct((3,) + tile, F32),
            jax.ShapeDtypeStruct(tile, F32),
        ],
        in_specs=[hbm] * 4 + [smem] * 3 + [hbm] * 4 + [smem] * 2,
        out_specs=[vmem] * 3,
        scratch_shapes=[
            pltpu.SMEM((2, doms), jnp.int32),
            pltpu.VMEM(tile, F32),
            pltpu.VMEM(tile, F32),
            pltpu.VMEM((3, GROUPS * LANES), F32),
            pltpu.VMEM(tile, F32),
            pltpu.VMEM(tile, F32),
            pltpu.VMEM((width, 6) + tile, F32),
            pltpu.VMEM((height - 1, 6) + tile, F32),
            pltpu.VMEM((height, 6) + tile, F32),
            pltpu.VMEM((tiles,) + tile, F32),
            pltpu.VMEM((STEPS, 2, 2) + tile, F32),
            pltpu.VMEM((STEPS, 2, 2) + tile, F32),
            pltpu.VMEM((4,) + tile, F32),
            pltpu.VMEM((held,) + tile, F32),
            pltpu.VMEM((2, reps, held) + tile, F32),
            pltpu.VMEM((2,) + tile, F32),
            pltpu.VMEM((doms, 32, GROUPS * LANES), BF16),
            pltpu.VMEM((doms, GROUPS * LANES, 32), BF16),
            pltpu.VMEM((doms, 16, GROUPS * LANES), BF16),
            pltpu.VMEM((2, GROUPS * 32, LANES), F32),
            pltpu.VMEM((4, GROUPS * 16, LANES), F32),
            pltpu.VMEM((tiles, LANES, 32), BF16),
            pltpu.VMEM((tiles, 32, LANES), BF16),
            pltpu.VMEM((tiles + 5, 32, LANES), BF16),
            pltpu.VMEM((tiles + 5, 16, LANES), BF16),
            pltpu.VMEM((tiles,) + tile, F32),
            pltpu.VMEM((slots, GROUPS * LANES, 2 * LANES), BF16),
            pltpu.VMEM((slots + 1,) + tile, F32),
            pltpu.VMEM((STEPS, plane) + tile, F32),
            pltpu.VMEM((STEPS, plane) + tile, F32),
            pltpu.VMEM((STEPS,) + tile, F32),
            pltpu.VMEM((STEPS, levels) + tile, F32),
            pltpu.VMEM((STEPS,) + tile, F32),
            pltpu.VMEM((STEPS, plane) + tile, F32),
            pltpu.VMEM(tile, F32),
            pltpu.VMEM(tile, F32),
            pair_sems, pair_sems, pair_sems, pair_sems, pair_sems, pair_sems,
            step_sems, step_sems, step_sems, step_sems, step_sems,
            pair_sems,
            pltpu.SemaphoreType.DMA((8,)),
        ],
        compiler_params=pltpu.CompilerParams(
            collective_id=0, has_side_effects=True, vmem_limit_bytes=64 * 1024 * 1024
        ),
    )(
        positions.reshape((3,) + tile), velocities.reshape((3,) + tile), square(charge), square(inverse_mass), pair_tiles, halo_tiles, owners.T,
        centres, square(widths), square(map_density), square(map_error), partner, decision,
    )
    outs = pl.pallas_call(
        write_out,
        out_shape=[jax.ShapeDtypeStruct(o.shape, F32) for o in outs],
        in_specs=[vmem] * 3,
        out_specs=[hbm] * 3,
        scratch_shapes=[pltpu.SemaphoreType.DMA((3,))],
    )(*outs)
    return outs[0].reshape(positions.shape), outs[1].reshape(velocities.shape), outs[2].reshape(GROUPS * LANES)


def solution(mesh):
    placed = (
        P("rep", None, "dom"),
        P("rep", None, "dom"),
        P("dom"),
        P("dom"),
        P("dom", None),
        P("dom", None, None),
        P("dom", None),
        P(None, "dom"),
        P("dom"),
        P("dom"),
        P("dom"),
        P(),
        P(),
    )
    return jax.shard_map(
        local,
        mesh=mesh,
        in_specs=placed,
        out_specs=(P("rep", None, "dom"), P("rep", None, "dom"), P("dom")),
        check_vma=False,
    )
```
